256 devices in a mesh: dp: 32 (over y_hi, z, core), tensor: 8 (over y_lo, x).
Axes of the slice: x: 4, y: 4 (y_hi: 2, y_lo: 2; y = y_hi * 2 + y_lo), z: 8, core: 2. Of those that a mesh axis runs over, the one named last changes fastest.
Arguments:
- teacher_q: bfloat16 [32, 1024, 8192], P('dp', None, 'tensor'), may hold values from -80 to 80
- teacher_k: bfloat16 [32, 1024, 1024], P('dp', None, 'tensor'), may hold values from -80 to 80
- teacher_v: bfloat16 [32, 1024, 1024], P('dp', None, 'tensor'), may hold values from -80 to 80
- student_q: bfloat16 [32, 1024, 2048], P('dp', 'tensor'), may hold values from -80 to 80
- student_k: bfloat16 [32, 1024, 256], P('dp', 'tensor'), may hold values from -80 to 80
- student_v: bfloat16 [32, 1024, 256], P('dp', 'tensor'), may hold values from -80 to 80
- lengths: int32 [32], replicated, may hold values from 1 to 1024, 24576 in all
- seq_weight: float32 [32], replicated, may hold values from 0.5 to 4
Outputs:
- relation_loss: float32 [32, 8], P('dp', 'tensor')
- student_q_grad: bfloat16 [32, 1024, 2048], P('dp', 'tensor')
- student_k_grad: bfloat16 [32, 1024, 256], P('dp', 'tensor')
- student_v_grad: bfloat16 [32, 1024, 256], P('dp', 'tensor')
The draws below stay inside these ranges and needn't reach their ends.
Inputs may be any that keep to these rules, and one draw needn't show every extreme that they name: Tokens at positions lengths[s] and after are padding of sequence s; some sequence has all 1024 tokens valid.
All inputs are finite; a program needn't handle non-finite values.
Results may differ from the reference program's by a relative error of at most 0.0036.
Values may be sent and summed in bfloat16 or wider, within the bound.
A program may use at most 64 MiB of HBM per device.

```python
import math
import jax
import jax.numpy as jnp
import numpy as np
from jax import lax

D_TQ = 8192
D_TKV = 1024
D_SQ = 2048
STUDENT_KV_WIDTH = 256
RELATION_COUNT = 64
SEQUENCE_TOKENS = 1024
SEQUENCE_COUNT = 32
N_TENSOR = 8


def reshaped_rows(key, full_shape, head_size, amplify_scale):
    normal_part = jnp.clip(jax.random.normal(jax.random.fold_in(key, 1), full_shape, jnp.float32), -4.0, 4.0)
    mixed = normal_part
    common = jnp.clip(jax.random.normal(jax.random.fold_in(key, 3), (full_shape[0], 1, full_shape[2]), jnp.float32), -3.0, 3.0)
    coefficient = jnp.clip(jax.random.normal(jax.random.fold_in(key, 4), (full_shape[0], full_shape[1], 1), jnp.float32), -2.0, 2.0)
    lifted_rows = jax.random.randint(jax.random.fold_in(key, 5), (full_shape[0], full_shape[1], 1), 0, 32) == 0
    lift_factor = jnp.where(lifted_rows, amplify_scale, 1.0)
    return ((mixed + 0.8 * coefficient * common) * head_size ** (-0.25) * lift_factor).astype(jnp.bfloat16)


def draw_teacher_q(key, part):
    key = jax.random.fold_in(key, 11)
    amplify_scale = 1.0
    return reshaped_rows(key, (SEQUENCE_COUNT, SEQUENCE_TOKENS, D_TQ), D_TQ // RELATION_COUNT, amplify_scale)


def draw_teacher_k(key, part):
    key = jax.random.fold_in(key, 12)
    amplify_scale = 1.0
    return reshaped_rows(key, (SEQUENCE_COUNT, SEQUENCE_TOKENS, D_TKV), D_TKV // RELATION_COUNT, amplify_scale)


def draw_teacher_v(key, part):
    key = jax.random.fold_in(key, 13)
    amplify_scale = 1.0
    return reshaped_rows(key, (SEQUENCE_COUNT, SEQUENCE_TOKENS, D_TKV), D_TKV // RELATION_COUNT, amplify_scale)


def draw_student_q(key, part):
    key = jax.random.fold_in(key, 14)
    amplify_scale = 1.0
    return reshaped_rows(key, (SEQUENCE_COUNT, SEQUENCE_TOKENS, D_SQ), D_SQ // RELATION_COUNT, amplify_scale)


def draw_student_k(key, part):
    key = jax.random.fold_in(key, 15)
    amplify_scale = 1.0
    return reshaped_rows(key, (SEQUENCE_COUNT, SEQUENCE_TOKENS, STUDENT_KV_WIDTH), STUDENT_KV_WIDTH // RELATION_COUNT, amplify_scale)


def draw_student_v(key, part):
    key = jax.random.fold_in(key, 16)
    amplify_scale = 1.0
    return reshaped_rows(key, (SEQUENCE_COUNT, SEQUENCE_TOKENS, STUDENT_KV_WIDTH), STUDENT_KV_WIDTH // RELATION_COUNT, amplify_scale)


def split_up(count, total, most, skew):
    loads = [(1 << 20) // math.isqrt(grade ** skew) + 1 for grade in range(2, count + 1)]
    surplus, given = total - most - (count - 1), [1] * (count - 1)
    while surplus > 0:
        candidates = [i for i in range(count - 1) if given[i] < most]
        mass, left = sum([loads[i] for i in candidates]), surplus
        for i in candidates:
            more = min(most - given[i], max(1, left * loads[i] // mass), surplus)
            given[i] = given[i] + more
            surplus = surplus - more
    return np.array([most] + given)


def ragged(stream_key, number_of, total, bound, skew):
    if number_of == 2:
        one = jax.random.randint(stream_key, (), max(1, total - bound), min(bound, total - 1) + 1)
        return jnp.stack([one, total - one])
    tallies = jnp.asarray(split_up(number_of, total, bound, skew), jnp.int32)
    pairs = (number_of - 1) // 2
    giver, sink = tallies[1:1 + 2 * pairs:2], tallies[2:2 + 2 * pairs:2]
    slack = jnp.minimum(giver - 1, bound - sink)
    shifted = jax.random.randint(jax.random.fold_in(stream_key, 1), (pairs,), 0, 1 << 20) % (slack + 1)
    tallies = tallies.at[1:1 + 2 * pairs:2].set(giver - shifted).at[2:2 + 2 * pairs:2].set(sink + shifted)
    return tallies[jax.random.permutation(jax.random.fold_in(stream_key, 2), number_of)]


def setup_inputs(seed: int = 0) -> dict:
    streams_of = jax.random.split(jax.random.key(seed), 9)
    return {
        "teacher_q": draw_teacher_q(jax.random.fold_in(streams_of[8], 71), 0),
        "teacher_k": draw_teacher_k(jax.random.fold_in(streams_of[8], 71), 0),
        "teacher_v": draw_teacher_v(jax.random.fold_in(streams_of[8], 71), 0),
        "student_q": draw_student_q(jax.random.fold_in(streams_of[8], 71), 0),
        "student_k": draw_student_k(jax.random.fold_in(streams_of[8], 71), 0),
        "student_v": draw_student_v(jax.random.fold_in(streams_of[8], 71), 0),
        "lengths": ragged(streams_of[6], SEQUENCE_COUNT, SEQUENCE_COUNT * SEQUENCE_TOKENS * 3 // 4, SEQUENCE_TOKENS, 2).astype(jnp.int32),
        "seq_weight": jnp.clip(jnp.exp(jax.random.uniform(streams_of[7], (SEQUENCE_COUNT,), jnp.float32, math.log(0.5), math.log(4.0))), 0.5, 4.0),
    }


def relation_terms(teach, stud, length, weight):
    seq_len = teach.shape[0]
    positions = jnp.arange(seq_len, dtype=jnp.int32)
    valid_keys = positions[None, :] < length
    valid_rows = positions < length
    teach_score = jnp.dot(teach, teach.T, preferred_element_type=jnp.float32) * (teach.shape[1] ** -0.5)
    stud_score = jnp.dot(stud, stud.T, preferred_element_type=jnp.float32) * (stud.shape[1] ** -0.5)
    teach_score = jnp.where(valid_keys, teach_score, -1e30)
    stud_score = jnp.where(valid_keys, stud_score, -1e30)
    log_teach = jax.nn.log_softmax(teach_score, axis=1)
    log_stud = jax.nn.log_softmax(stud_score, axis=1)
    prob_teach = jnp.exp(log_teach)
    prob_stud = jnp.exp(log_stud)
    row_divergence = jnp.sum(jnp.where(valid_keys, prob_teach * (log_teach - log_stud), 0.0), axis=1)
    kl_total = jnp.sum(jnp.where(valid_rows, row_divergence, 0.0))
    slope_rows = jnp.where(valid_rows[:, None], weight * (prob_stud - prob_teach), 0.0).astype(jnp.bfloat16)
    gradient = jnp.dot(slope_rows, stud, preferred_element_type=jnp.float32)
    gradient = gradient + jnp.dot(slope_rows.T, stud, preferred_element_type=jnp.float32)
    return kl_total, gradient * (stud.shape[1] ** -0.5)


def by_head(values):
    return values.reshape(values.shape[0], RELATION_COUNT, values.shape[1] // RELATION_COUNT).transpose(1, 0, 2)


def merged(values):
    return values.transpose(1, 0, 2).reshape(values.shape[1], -1).astype(jnp.bfloat16)


def reference(teacher_q, teacher_k, teacher_v, student_q, student_k, student_v, lengths, seq_weight):
    def one_seq(seq_items):
        teach_q, teach_k, teach_v, stud_q, stud_k, stud_v, length, weight = seq_items

        def one_head(head_items):
            kl_head = jnp.zeros((), jnp.float32)
            gradients = []
            for kind_index in range(3):
                part_loss, gradient = relation_terms(head_items[kind_index], head_items[3 + kind_index], length, weight)
                kl_head = kl_head + part_loss
                gradients.append(gradient)
            return kl_head, gradients[0], gradients[1], gradients[2]

        head_loss, grad_q, grad_k, grad_v = lax.map(one_head, tuple(by_head(values) for values in (teach_q, teach_k, teach_v, stud_q, stud_k, stud_v)))
        group_loss = head_loss.reshape(N_TENSOR, -1).sum(axis=1) / length.astype(jnp.float32)
        return group_loss, merged(grad_q), merged(grad_k), merged(grad_v)

    relation_loss, student_q_grad, student_k_grad, student_v_grad = lax.map(one_seq, (teacher_q, teacher_k, teacher_v, student_q, student_k, student_v, lengths, seq_weight))
    return (relation_loss, student_q_grad, student_k_grad, student_v_grad)
```

```python
import functools
import math

import jax
import jax.numpy as jnp
from jax import lax
from jax.experimental import pallas as pl
from jax.experimental.pallas import tpu as pltpu
from jax.sharding import PartitionSpec as P

bf16, f32 = jnp.bfloat16, jnp.float32
MESH = pl.DeviceIdType.MESH
NT = (((1,), (1,)), ((), ()))
NN = (((1,), (0,)), ((), ()))
N = 1024
TS = 8
ROWS = N // TS
HEADS = 8
BL = 256
NB = N // BL
LOG2E = math.log2(math.e)
SAFE_LOG2 = 115.0
VMEM_LIMIT = 60 * 2**20


def dot(a, b, dims):
    return lax.dot_general(a, b, dims, preferred_element_type=f32)


def fold_kv(k, v):
    h = ROWS // 2
    return jnp.concatenate([k[:h], v[:h], k[h:], v[h:]], axis=1)


def greet(me):
    barrier = pltpu.get_barrier_semaphore()
    for s in range(1, TS):
        pl.semaphore_signal(
            barrier, inc=1, device_id={"tensor": lax.rem(me + s, TS)}, device_id_type=MESH
        )
    pl.semaphore_wait(barrier, TS - 1)


def send(src, dst, send_sem, recv_sem, peer):
    return pltpu.make_async_remote_copy(
        src_ref=src,
        dst_ref=dst,
        send_sem=send_sem,
        recv_sem=recv_sem,
        device_id={"tensor": peer},
        device_id_type=MESH,
    )


def forward_kernel(sq, sk, sv, rq, rkv, kv, send_sem, recv_sem, own_sem):
    me = lax.axis_index("tensor")
    for t in range(TS):
        kv[t] = fold_kv(sk[0, :, t * 32 : t * 32 + 32], sv[0, :, t * 32 : t * 32 + 32])
    greet(me)

    def parts(t):
        return (
            (sq.at[0, :, pl.ds(pl.multiple_of(t * 256, 256), 256)],
             rq.at[pl.ds(pl.multiple_of(me * ROWS, ROWS), ROWS), :]),
            (kv.at[t], rkv.at[me]),
        )

    copies = []
    for s in range(1, TS):
        peer = lax.rem(me + s, TS)
        for i, (src, dst) in enumerate(parts(peer)):
            copies.append(send(src, dst, send_sem.at[i, s], recv_sem.at[i, s], peer))
            copies[-1].start()
    own = [
        pltpu.make_async_copy(src, dst, own_sem.at[i])
        for i, (src, dst) in enumerate(parts(me))
    ]
    for c in own:
        c.start()
    for c in own:
        c.wait()
    for c in copies:
        c.wait()


def forward(sq, sk, sv):
    return pl.pallas_call(
        forward_kernel,
        out_shape=(
            jax.ShapeDtypeStruct((N, 256), bf16),
            jax.ShapeDtypeStruct((TS, ROWS // 2, 128), bf16),
        ),
        in_specs=[pl.BlockSpec(memory_space=pltpu.VMEM)] * 3,
        out_specs=[pl.BlockSpec(memory_space=pltpu.VMEM)] * 2,
        scratch_shapes=[
            pltpu.VMEM((TS, ROWS // 2, 128), bf16),
            pltpu.SemaphoreType.DMA((2, TS)),
            pltpu.SemaphoreType.DMA((2, TS)),
            pltpu.SemaphoreType.DMA((2,)),
        ],
        compiler_params=pltpu.CompilerParams(collective_id=0, has_side_effects=True),
    )(sq, sk, sv)


def backward_kernel(gq, gkv, oq, ok, ov, kv, send_sem, recv_sem, own_sem):
    me = lax.axis_index("tensor")
    greet(me)

    def parts(t):
        return (
            (gq.at[pl.ds(pl.multiple_of(t * ROWS, ROWS), ROWS), :],
             oq.at[0, :, pl.ds(pl.multiple_of(me * 256, 256), 256)]),
            (gkv.at[t], kv.at[me]),
        )

    copies = []
    for s in range(1, TS):
        peer = lax.rem(me + s, TS)
        for i, (src, dst) in enumerate(parts(peer)):
            copies.append(send(src, dst, send_sem.at[i, s], recv_sem.at[i, s], peer))
            copies[-1].start()
    own = [
        pltpu.make_async_copy(src, dst, own_sem.at[i])
        for i, (src, dst) in enumerate(parts(me))
    ]
    for c in own:
        c.start()
    for c in own:
        c.wait()
    for c in copies:
        c.wait()
    h = ROWS // 2
    for i, out in enumerate((ok, ov)):
        for half in range(2):
            lo = half * 64 + i * 32
            out[0, half * h : half * h + h, :] = jnp.concatenate(
                [kv[t][:, lo : lo + 32] for t in range(TS)], axis=1
            )


def backward(gq, gkv):
    return pl.pallas_call(
        backward_kernel,
        out_shape=(
            jax.ShapeDtypeStruct((1, ROWS, 2048), bf16),
            jax.ShapeDtypeStruct((1, ROWS, 256), bf16),
            jax.ShapeDtypeStruct((1, ROWS, 256), bf16),
        ),
        in_specs=[pl.BlockSpec(memory_space=pltpu.VMEM)] * 2,
        out_specs=[pl.BlockSpec(memory_space=pltpu.VMEM)] * 3,
        scratch_shapes=[
            pltpu.VMEM((TS, ROWS // 2, 128), bf16),
            pltpu.SemaphoreType.DMA((2, TS)),
            pltpu.SemaphoreType.DMA((2, TS)),
            pltpu.SemaphoreType.DMA((2,)),
        ],
        compiler_params=pltpu.CompilerParams(collective_id=1, has_side_effects=True),
    )(gq, gkv)


class Head:
    def __init__(self, n):
        q = n < HEADS
        kv = jnp.where(n < 2 * HEADS, 0, 1)
        sub = lax.rem(n, HEADS)
        self.t_at = pl.multiple_of(jnp.where(q, n, HEADS + kv) * 128, 128)
        self.s_at = pl.multiple_of(jnp.where(q, n // 4, 2 + kv) * 128, 128)
        self.g_at = pl.multiple_of(jnp.where(q, 32 * n, 256 + 32 * kv), 32)
        self.t_scale = jnp.where(q, LOG2E * 128**-0.5, LOG2E * 0.25).astype(f32)
        self.s_scale = jnp.where(q, LOG2E * 32**-0.5, LOG2E * 0.5).astype(f32)
        self.g_scale = jnp.where(q, 32**-0.5, 0.5).astype(f32)
        self.t_lo = jnp.where(q, 0, 16 * sub)
        self.t_hi = jnp.where(q, 128, 16 * sub + 16)
        self.s_lo = jnp.where(q, 32 * lax.rem(n, 4), 4 * sub)
        self.s_hi = self.s_lo + jnp.where(q, 32, 4)
        self.b_lo = jnp.where(q, 0, 4 * sub)
        self.b_hi = jnp.where(q, 32, 4 * sub + 4)


def setup(length, tq, tk, tv, rq, rkv, ta, sb, bt, grad):
    valid = lax.broadcasted_iota(jnp.int32, (N, 1), 0) < length

    def real(x):
        return jnp.where(valid, x.astype(f32), 0.0)

    ta[:, 0:1024] = real(tq[0]).astype(bf16)
    ta[:, 1024:1152] = real(tk[0]).astype(bf16)
    ta[:, 1152:1280] = real(tv[0]).astype(bf16)
    b = real(rq[...])
    sb[:, 0:256] = b.astype(bf16)
    bt[0:256] = b.T.astype(bf16)
    folded = rkv[...]
    for i in range(2):
        halves = [folded[:, :, 64 * h + 32 * i : 64 * h + 32 * i + 32] for h in range(2)]
        b = jnp.concatenate(halves, axis=1).reshape(N, 32)
        b = real(jnp.concatenate([b, jnp.zeros((N, 96), bf16)], axis=1))
        sb[:, 256 + 128 * i : 384 + 128 * i] = b.astype(bf16)
        bt[256 + 32 * i : 288 + 32 * i] = b.T[0:32].astype(bf16)
    grad[...] = jnp.zeros_like(grad)


def largest(x):
    return jnp.max(jnp.abs(x).astype(f32))


def scores_bound(ta, sb):
    def bound(x, w):
        top = largest(x)
        return (LOG2E * 1.0001 * w**0.5) * top * top

    return jnp.maximum(
        jnp.maximum(bound(ta[:, 0:1024], 128), bound(ta[:, 1024:1280], 16)),
        jnp.maximum(bound(sb[:, 0:256], 32), bound(sb[:, 256:512], 4)),
    )


def head_operands(h, ta, sb, lt, rt, ls, rs):
    lane = lax.broadcasted_iota(jnp.int32, (1, 128), 1)

    def put(x, scale, lo, hi, left, right):
        xf = x.astype(f32)
        right[...] = jnp.where((lane >= lo) & (lane < hi), xf, 0.0).astype(bf16)
        y = xf * scale
        top = y.astype(bf16)
        left[:, 0:128] = top
        left[:, 128:256] = (y - top.astype(f32)).astype(bf16)

    put(ta[:, pl.ds(h.t_at, 128)], h.t_scale, h.t_lo, h.t_hi, lt, rt)
    put(sb[:, pl.ds(h.s_at, 128)], h.s_scale, h.s_lo, h.s_hi, ls, rs)


def head_columns(h, bt, at=slice(None)):
    sub = lax.broadcasted_iota(jnp.int32, (32, 1), 0)
    b = bt[pl.ds(h.g_at, 32), at].astype(f32)
    return jnp.where((sub >= h.b_lo) & (sub < h.b_hi), b, 0.0).astype(bf16)


def folded_sum(x):
    return x.reshape(x.shape[0] // 8, 8, x.shape[1]).sum(0)


def first_block(i, j, lt, rt, ls, rs, et, es, diff, row_t, row_s, col):
    ri, rj = pl.ds(i * BL, BL), pl.ds(j * BL, BL)
    x_t = dot(lt[ri], jnp.concatenate([rt[rj], rt[rj]], axis=1), NT)
    x_s = dot(ls[ri], jnp.concatenate([rs[rj], rs[rj]], axis=1), NT)
    e_t, e_s = jnp.exp2(x_t), jnp.exp2(x_s)
    et[ri, rj] = e_t
    es[ri, rj] = e_s
    diff[ri, rj] = x_t - x_s
    if i == 0:
        col[0:8, rj] = folded_sum(e_t)
        col[8:16, rj] = folded_sum(e_s)
    else:
        col[0:8, rj] += folded_sum(e_t)
        col[8:16, rj] += folded_sum(e_s)
    if j == i + 1:
        row_t[ri] = e_t[:, :128] + e_t[:, 128:]
        row_s[ri] = e_s[:, :128] + e_s[:, 128:]
    elif j > i:
        row_t[ri] += e_t[:, :128] + e_t[:, 128:]
        row_s[ri] += e_s[:, :128] + e_s[:, 128:]


def row_statistics(length, row_t, row_s, col, rvec, rb_t, rb_s, log_sum):
    valid = lax.broadcasted_iota(jnp.int32, (1, N), 1) < length
    padded = (N - length).astype(f32)

    def total(row, c):
        r = jnp.sum(row[0 : N - BL].T, axis=0, keepdims=True)
        r = jnp.concatenate([r, jnp.zeros((1, BL), f32)], axis=1)
        return jnp.where(valid, r + jnp.sum(c, axis=0, keepdims=True) - padded, 1.0)

    sum_t, sum_s = total(row_t, col[0:8]), total(row_s, col[8:16])
    r_t, r_s = jnp.where(valid, 1.0 / sum_t, 0.0), jnp.where(valid, 1.0 / sum_s, 0.0)
    rvec[0:8] = jnp.broadcast_to(r_t, (8, N))
    rvec[8:16] = jnp.broadcast_to(r_s, (8, N))
    rb_t[...] = jnp.broadcast_to(r_t, (128, N)).T
    rb_s[...] = jnp.broadcast_to(r_s, (128, N)).T
    log_sum[0:1, :] += jnp.log2(sum_s) - jnp.log2(sum_t)


def second_block(i, j, et, es, diff, rvec, rb_t, rb_s, both, kl):
    ri, rj = pl.ds(i * BL, BL), pl.ds(j * BL, BL)

    def pair(by_row, by_col):
        wide = jnp.concatenate([by_row, by_row], axis=1).reshape(BL // 8, 8, BL)
        return (wide + by_col[None]).reshape(BL, BL)

    q_t = et[ri, rj] * pair(rb_t[ri], rvec[0:8, rj])
    both[ri, rj] = (es[ri, rj] * pair(rb_s[ri], rvec[8:16, rj]) - q_t).astype(bf16)
    part = folded_sum(q_t * diff[ri, rj])
    kl[:, rj] += 0.5 * part if i == j else part


def bounded_heads(length, weight, ta, sb, bt, grad, lt, rt, ls, rs, et, es, diff, row_t, row_s, col, rvec, rb_t, rb_s, both, kl, log_sum):
    def one_head(n, carry):
        h = Head(n)
        head_operands(h, ta, sb, lt, rt, ls, rs)
        for j in range(NB):
            for i in range(j + 1):
                first_block(i, j, lt, rt, ls, rs, et, es, diff, row_t, row_s, col)
        row_statistics(length, row_t, row_s, col, rvec, rb_t, rb_s, log_sum)
        for j in range(NB):
            for i in range(j + 1):
                second_block(i, j, et, es, diff, rvec, rb_t, rb_s, both, kl)
        b = head_columns(h, bt)
        scale = h.g_scale * weight
        for j in range(NB):
            lo, hi = j * BL, (j + 1) * BL
            g = dot(b[:, :hi], both[0:hi, lo:hi], NN)
            if hi < N:
                g = g + dot(b[:, hi:], both[lo:hi, hi:N], NT)
            grad[pl.ds(h.g_at, 32), lo:hi] += g * scale
        return carry

    lax.fori_loop(0, 3 * HEADS, one_head, 0)


def general_heads(length, weight, ta, sb, bt, grad, rt, rs, lt, ls, both, kl, strip=128):
    keys = lax.broadcasted_iota(jnp.int32, (1, N), 1) < length

    def one_head(n, carry):
        h = Head(n)
        head_operands(h, ta, sb, lt, rt, ls, rs)
        b = head_columns(h, bt)
        scale = h.g_scale * weight

        def rows(k, carry):
            at = pl.ds(pl.multiple_of(k * strip, strip), strip)
            here = k * strip + lax.broadcasted_iota(jnp.int32, (strip, 1), 0) < length

            def softmax(x, c):
                x = jnp.where(keys, dot(x[at], x[...], NT) * c, -1e30)
                x = x - jnp.max(x, axis=1, keepdims=True)
                x = x - jnp.log2(jnp.sum(jnp.exp2(x), axis=1, keepdims=True))
                return x, jnp.exp2(x)

            log_t, p_t = softmax(rt, h.t_scale)
            log_s, p_s = softmax(rs, h.s_scale)
            inside = keys & here
            kl[...] += folded_sum(jnp.where(inside, p_t * (log_t - log_s), 0.0))
            slope = jnp.where(inside, p_s - p_t, 0.0).astype(bf16)
            both[at, :] = slope
            grad[pl.ds(h.g_at, 32), :] += dot(head_columns(h, bt, at), slope, NN) * scale
            grad[pl.ds(h.g_at, 32), at] += dot(b, slope, NT) * scale
            return carry

        return lax.fori_loop(0, N // strip, rows, carry)

    lax.fori_loop(0, 3 * HEADS, one_head, 0)


def heads_kernel(
    lengths, weights, tq, tk, tv, rq, rkv, loss, gq, gkv,
    ta, sb, bt, grad, lt, rt, ls, rs, et, es, diff, row_t, row_s, col, rvec, rb_t, rb_s, both, kl, log_sum,
):
    owner = lax.axis_index("dp")
    length, weight = lengths[owner], weights[owner]
    setup(length, tq, tk, tv, rq, rkv, ta, sb, bt, grad)
    kl[...] = jnp.zeros_like(kl)
    log_sum[...] = jnp.zeros_like(log_sum)
    bounded = scores_bound(ta, sb) <= SAFE_LOG2

    @pl.when(bounded)
    def _():
        bounded_heads(length, weight, ta, sb, bt, grad, lt, rt, ls, rs, et, es, diff, row_t, row_s, col, rvec, rb_t, rb_s, both, kl, log_sum)

    @pl.when(jnp.logical_not(bounded))
    def _():
        general_heads(length, weight, ta, sb, bt, grad, rt, rs, lt, ls, both, kl)

    total = (jnp.sum(kl[...]) + jnp.sum(log_sum[...])) * math.log(2.0)
    loss[0, 0] = total / length.astype(f32)
    valid = lax.broadcasted_iota(jnp.int32, (N, 1), 0) < length
    gq[...] = jnp.where(valid, grad[0:256].T, 0.0).astype(bf16)
    kv = jnp.concatenate([grad[256:320], jnp.zeros((64, N), f32)], axis=0).T
    kv = jnp.where(valid, kv, 0.0).astype(bf16).reshape(TS, 2, ROWS // 2, 128)
    gkv[...] = jnp.concatenate([kv[:, 0, :, 0:64], kv[:, 1, :, 0:64]], axis=2)


def heads(lengths, weights, tq, tk, tv, rq, rkv):
    smem = pl.BlockSpec(memory_space=pltpu.SMEM)
    vmem = pl.BlockSpec(memory_space=pltpu.VMEM)
    square = (N, N)
    return pl.pallas_call(
        heads_kernel,
        out_shape=(
            jax.ShapeDtypeStruct((1, 1), f32),
            jax.ShapeDtypeStruct((N, 256), bf16),
            jax.ShapeDtypeStruct((TS, ROWS // 2, 128), bf16),
        ),
        in_specs=[smem, smem] + [vmem] * 5,
        out_specs=[smem, vmem, vmem],
        scratch_shapes=[
            pltpu.VMEM((N, 1280), bf16),
            pltpu.VMEM((N, 512), bf16),
            pltpu.VMEM((320, N), bf16),
            pltpu.VMEM((320, N), f32),
            pltpu.VMEM((N, 256), bf16),
            pltpu.VMEM((N, 128), bf16),
            pltpu.VMEM((N, 256), bf16),
            pltpu.VMEM((N, 128), bf16),
            pltpu.VMEM(square, f32),
            pltpu.VMEM(square, f32),
            pltpu.VMEM(square, f32),
            pltpu.VMEM((N, 128), f32),
            pltpu.VMEM((N, 128), f32),
            pltpu.VMEM((16, N), f32),
            pltpu.VMEM((16, N), f32),
            pltpu.VMEM((N, 128), f32),
            pltpu.VMEM((N, 128), f32),
            pltpu.VMEM(square, bf16),
            pltpu.VMEM((8, N), f32),
            pltpu.VMEM((8, N), f32),
        ],
        compiler_params=pltpu.CompilerParams(vmem_limit_bytes=VMEM_LIMIT),
    )(lengths, weights, tq, tk, tv, rq, rkv)


def on_device(teacher_q, teacher_k, teacher_v, student_q, student_k, student_v, lengths, seq_weight):
    rq, rkv = forward(student_q, student_k, student_v)
    loss, gq, gkv = heads(lengths, seq_weight, teacher_q, teacher_k, teacher_v, rq, rkv)
    return (loss, *backward(gq, gkv))


def solution(mesh):
    in_specs = (
        P("dp", None, "tensor"),
        P("dp", None, "tensor"),
        P("dp", None, "tensor"),
        P("dp", "tensor", None),
        P("dp", "tensor", None),
        P("dp", "tensor", None),
        P(),
        P(),
    )
    out_specs = (
        P("dp", "tensor"),
        P("dp", "tensor", None),
        P("dp", "tensor", None),
        P("dp", "tensor", None),
    )
    return jax.shard_map(
        on_device, mesh=mesh, in_specs=in_specs, out_specs=out_specs, check_vma=False
    )
```

```python
import functools
import math

import jax
import jax.numpy as jnp
from jax import lax
from jax.experimental import pallas as pl
from jax.experimental.pallas import tpu as pltpu
from jax.sharding import PartitionSpec as P

bf16, f32 = jnp.bfloat16, jnp.float32
MESH = pl.DeviceIdType.MESH
NT = (((1,), (1,)), ((), ()))
NN = (((1,), (0,)), ((), ()))
N = 1024
TS = 8
ROWS = N // TS
HALF = ROWS // 2
HEADS = 8
BL = 256
NB = N // BL
LOG2E = math.log2(math.e)
SAFE_LOG2 = 115.0
VMEM_LIMIT = 60 * 2**20


RELATION_COUNT = 64


def as_sent(value):
    return jax.tree.map(lambda a: a.astype(jnp.bfloat16) if a.dtype == jnp.float32 else a, value)


def head_terms(teach, stud, length, weight):
    seq_len = teach.shape[0]
    block_rows = min(512, seq_len)
    teach_scale = teach.shape[1] ** (-0.5)
    stud_scale = stud.shape[1] ** (-0.5)
    key_positions = jnp.arange(seq_len, dtype=jnp.int32)
    valid_keys = key_positions[None, :] < length
    kl_total = jnp.zeros((), jnp.float32)
    across = jnp.zeros(stud.shape, jnp.float32)
    row_parts = []
    for row_start in range(0, seq_len, block_rows):
        teach_rows = teach[row_start : row_start + block_rows]
        stud_rows = stud[row_start : row_start + block_rows]
        teach_score = jnp.dot(teach_rows, teach.T, preferred_element_type=jnp.float32) * teach_scale
        stud_score = jnp.dot(stud_rows, stud.T, preferred_element_type=jnp.float32) * stud_scale
        teach_score = jnp.where(valid_keys, teach_score, -1e30)
        stud_score = jnp.where(valid_keys, stud_score, -1e30)
        log_teach = jax.nn.log_softmax(teach_score, axis=1)
        log_stud = jax.nn.log_softmax(stud_score, axis=1)
        prob_teach = jnp.exp(log_teach)
        prob_stud = jnp.exp(log_stud)
        valid_rows = row_start + jnp.arange(block_rows, dtype=jnp.int32) < length
        row_divergence = jnp.sum(
            jnp.where(valid_keys, prob_teach * (log_teach - log_stud), 0.0), axis=1
        )
        kl_total = kl_total + jnp.sum(jnp.where(valid_rows, row_divergence, 0.0))
        slope_rows = jnp.where(valid_rows[:, None], weight * (prob_stud - prob_teach), 0.0).astype(
            jnp.bfloat16
        )
        row_parts.append(jnp.dot(slope_rows, stud, preferred_element_type=jnp.float32))
        across = across + lax.dot_general(
            slope_rows, stud_rows, (((0,), (0,)), ((), ())), preferred_element_type=jnp.float32
        )
    gradient = ((jnp.concatenate(row_parts, axis=0) + across) * stud_scale).astype(jnp.bfloat16)
    return (kl_total, gradient)


def kind_pass(teach_heads, stud_heads, length, weight):

    def one_head(head_pair):
        return head_terms(head_pair[0], head_pair[1], length, weight)

    head_losses, gradients = lax.map(one_head, (teach_heads, stud_heads))
    return (jnp.sum(head_losses), gradients)


def split_heads(values, head_count):
    return values.reshape(values.shape[0], head_count, values.shape[1] // head_count).transpose(
        1, 0, 2
    )


def general_program(
    teacher_q, teacher_k, teacher_v, student_q, student_k, student_v, lengths, seq_weight
):
    tensor_size = lax.axis_size("tensor")
    head_count = RELATION_COUNT // tensor_size
    owner_index = lax.axis_index("dp")
    length = lax.dynamic_index_in_dim(lengths, owner_index, 0, keepdims=False)
    weight = lax.dynamic_index_in_dim(seq_weight, owner_index, 0, keepdims=False)
    seq_len = teacher_q.shape[1]

    def spread(values):
        return values.reshape(
            values.shape[0], values.shape[1], tensor_size, values.shape[2] // tensor_size
        )

    def settle(values):
        return split_heads(values.reshape(seq_len, values.shape[3]), head_count)

    def gather_back(gradients):
        return gradients.transpose(1, 0, 2).reshape(1, seq_len, 1, -1)

    def restore(values):
        return values.reshape(values.shape[0], values.shape[1], values.shape[2] * values.shape[3])

    teach_queries = split_heads(teacher_q[0], head_count)
    teach_keys = split_heads(teacher_k[0], head_count)
    teach_values = split_heads(teacher_v[0], head_count)
    got_queries, got_keys, got_values = (
        lax.all_to_all(spread(student_q), "tensor", split_axis=2, concat_axis=1, tiled=True),
        lax.all_to_all(spread(student_k), "tensor", split_axis=2, concat_axis=1, tiled=True),
        lax.all_to_all(spread(student_v), "tensor", split_axis=2, concat_axis=1, tiled=True),
    )
    query_loss, query_grads = kind_pass(teach_queries, settle(got_queries), length, weight)
    key_loss, key_grads = kind_pass(teach_keys, settle(got_keys), length, weight)
    value_loss, value_grads = kind_pass(teach_values, settle(got_values), length, weight)
    query_back, key_back, value_back = (
        lax.all_to_all(
            as_sent(gather_back(query_grads)), "tensor", split_axis=1, concat_axis=2, tiled=True
        ),
        lax.all_to_all(
            as_sent(gather_back(key_grads)), "tensor", split_axis=1, concat_axis=2, tiled=True
        ),
        lax.all_to_all(
            as_sent(gather_back(value_grads)), "tensor", split_axis=1, concat_axis=2, tiled=True
        ),
    )
    kl_sum = query_loss + key_loss + value_loss
    relation_loss = (kl_sum / length.astype(jnp.float32)).reshape(1, 1)
    return (relation_loss, restore(query_back), restore(key_back), restore(value_back))


def bound_lanes(x, w):
    top = jnp.max(jnp.abs(x).astype(f32).reshape(N // 8, 8, x.shape[1]), axis=0)
    top = functools.reduce(jnp.maximum, [top[:, c : c + 128] for c in range(0, x.shape[1], 128)])
    return (LOG2E * 1.0001 * w**0.5) * top * top


def dot(a, b, dims):
    return lax.dot_general(a, b, dims, preferred_element_type=f32)


def fold_kv(k, v):
    return jnp.concatenate([k[:HALF], v[:HALF], k[HALF:], v[HALF:]], axis=1)


class Head:
    def __init__(self, n):
        q = (n >= HEADS) & (n < 2 * HEADS)
        kv = jnp.where(n < HEADS, 0, 1)
        sub = lax.rem(n, HEADS)
        self.t_at = pl.multiple_of(jnp.where(q, sub, HEADS + kv) * 128, 128)
        self.s_at = pl.multiple_of(jnp.where(q, sub // 4, 2 + kv) * 128, 128)
        self.g_at = pl.multiple_of(jnp.where(q, 32 * sub, 256 + 32 * kv), 32)
        self.t_scale = jnp.where(q, LOG2E * 128**-0.5, LOG2E * 0.25).astype(f32)
        self.s_scale = jnp.where(q, LOG2E * 32**-0.5, LOG2E * 0.5).astype(f32)
        self.g_scale = jnp.where(q, 32**-0.5, 0.5).astype(f32)
        self.t_lo = jnp.where(q, 0, 16 * sub)
        self.t_hi = jnp.where(q, 128, 16 * sub + 16)
        self.s_lo = jnp.where(q, 32 * lax.rem(sub, 4), 4 * sub)
        self.s_hi = self.s_lo + jnp.where(q, 32, 4)
        self.b_lo = jnp.where(q, 0, 4 * sub)
        self.b_hi = jnp.where(q, 32, 4 * sub + 4)


def split_scaled(x, scale, left, at):
    y = x.astype(f32) * scale
    top = y.astype(bf16)
    left[:, at : at + 128] = top
    left[:, at + 128 : at + 256] = (y - top.astype(f32)).astype(bf16)


def set_teacher(valid, ta, lt):
    for g in range(HEADS + 2):
        at = g * 128
        x = jnp.where(valid, ta[:, at : at + 128].astype(f32), 0.0).astype(bf16)
        ta[:, at : at + 128] = x
        split_scaled(x, LOG2E * (128**-0.5 if g < HEADS else 0.25), lt, 2 * at)


def set_student_kv(valid, rkv, sb, bt, ls):
    folded = rkv[...]
    for i in range(2):
        halves = [folded[:, :, 64 * h + 32 * i : 64 * h + 32 * i + 32] for h in range(2)]
        b = jnp.concatenate(halves, axis=1).reshape(N, 32)
        b = jnp.where(valid, jnp.concatenate([b, jnp.zeros((N, 96), bf16)], axis=1).astype(f32), 0.0)
        at = 256 + 128 * i
        sb[:, at : at + 128] = b.astype(bf16)
        bt[256 + 32 * i : 288 + 32 * i] = b.T[0:32].astype(bf16)
        split_scaled(b.astype(bf16), LOG2E * 0.5, ls, 2 * at)


def set_student_q(valid, rq, sb, bt, ls):
    for g in range(2):
        at = 128 * g
        b = jnp.where(valid, rq[:, at : at + 128].astype(f32), 0.0)
        sb[:, at : at + 128] = b.astype(bf16)
        bt[at : at + 128] = b.T.astype(bf16)
        split_scaled(b.astype(bf16), LOG2E * 32**-0.5, ls, 2 * at)


def right_operands(h, ta, sb, rt, rs):
    lane = lax.broadcasted_iota(jnp.int32, (1, 128), 1)

    def keep(lo, hi):
        return ((lane >= lo) & (lane < hi)).astype(f32).astype(bf16)

    rt[...] = ta[:, pl.ds(h.t_at, 128)] * keep(h.t_lo, h.t_hi)
    rs[...] = sb[:, pl.ds(h.s_at, 128)] * keep(h.s_lo, h.s_hi)


def head_columns(h, bt):
    sub = lax.broadcasted_iota(jnp.int32, (32, 1), 0)
    b = bt[pl.ds(h.g_at, 32), :].astype(f32)
    return jnp.where((sub >= h.b_lo) & (sub < h.b_hi), b, 0.0).astype(bf16)


def folded_sum(x):
    return x.reshape(x.shape[0] // 8, 8, x.shape[1]).sum(0)


def first_block(i, j, h, lt, rt, ls, rs, et, es, diff, row_t, row_s, col):
    ri, rj = pl.ds(i * BL, BL), pl.ds(j * BL, BL)
    x_t = dot(lt[ri, pl.ds(2 * h.t_at, 256)], jnp.concatenate([rt[rj], rt[rj]], axis=1), NT)
    x_s = dot(ls[ri, pl.ds(2 * h.s_at, 256)], jnp.concatenate([rs[rj], rs[rj]], axis=1), NT)
    e_t, e_s = jnp.exp2(x_t), jnp.exp2(x_s)
    et[ri, rj] = e_t
    es[ri, rj] = e_s
    diff[ri, rj] = x_t - x_s
    if i == 0:
        col[0:8, rj] = folded_sum(e_t)
        col[8:16, rj] = folded_sum(e_s)
    else:
        col[0:8, rj] += folded_sum(e_t)
        col[8:16, rj] += folded_sum(e_s)
    if j == i + 1:
        row_t[ri] = e_t[:, :128] + e_t[:, 128:]
        row_s[ri] = e_s[:, :128] + e_s[:, 128:]
    elif j > i:
        row_t[ri] += e_t[:, :128] + e_t[:, 128:]
        row_s[ri] += e_s[:, :128] + e_s[:, 128:]


def row_statistics(length, row_t, row_s, col, rvec, rb_t, rb_s, log_sum):
    valid = lax.broadcasted_iota(jnp.int32, (1, N), 1) < length
    padded = (N - length).astype(f32)

    def total(row, c):
        r = jnp.sum(row[0 : N - BL].T, axis=0, keepdims=True)
        r = jnp.concatenate([r, jnp.zeros((1, BL), f32)], axis=1)
        return jnp.where(valid, r + jnp.sum(c, axis=0, keepdims=True) - padded, 1.0)

    sum_t, sum_s = total(row_t, col[0:8]), total(row_s, col[8:16])
    r_t, r_s = jnp.where(valid, 1.0 / sum_t, 0.0), jnp.where(valid, 1.0 / sum_s, 0.0)
    rvec[0:8] = jnp.broadcast_to(r_t, (8, N))
    rvec[8:16] = jnp.broadcast_to(r_s, (8, N))
    rb_t[...] = jnp.broadcast_to(r_t, (128, N)).T
    rb_s[...] = jnp.broadcast_to(r_s, (128, N)).T
    log_sum[0:1, :] += jnp.log2(sum_s) - jnp.log2(sum_t)


def second_block(i, j, et, es, diff, rvec, rb_t, rb_s, both, kl):
    ri, rj = pl.ds(i * BL, BL), pl.ds(j * BL, BL)

    def pair(by_row, by_col):
        wide = jnp.concatenate([by_row, by_row], axis=1).reshape(BL // 8, 8, BL)
        return (wide + by_col[None]).reshape(BL, BL)

    q_t = et[ri, rj] * pair(rb_t[ri], rvec[0:8, rj])
    both[ri, rj] = (es[ri, rj] * pair(rb_s[ri], rvec[8:16, rj]) - q_t).astype(bf16)
    part = folded_sum(q_t * diff[ri, rj])
    kl[:, rj] += 0.5 * part if i == j else part


def one_head(n, length, weight, ta, sb, bt, grad, lt, rt, ls, rs, et, es, diff, row_t, row_s, col, rvec, rb_t, rb_s, both, kl, log_sum):
    h = Head(n)
    right_operands(h, ta, sb, rt, rs)
    for j in range(NB):
        for i in range(j + 1):
            first_block(i, j, h, lt, rt, ls, rs, et, es, diff, row_t, row_s, col)
    row_statistics(length, row_t, row_s, col, rvec, rb_t, rb_s, log_sum)
    for j in range(NB):
        for i in range(j + 1):
            second_block(i, j, et, es, diff, rvec, rb_t, rb_s, both, kl)
    b = head_columns(h, bt)
    scale = h.g_scale * weight
    for j in range(NB):
        lo, hi = j * BL, (j + 1) * BL
        g = dot(b[:, :hi], both[0:hi, lo:hi], NN)
        if hi < N:
            g = g + dot(b[:, hi:], both[lo:hi, hi:N], NT)
        grad[pl.ds(h.g_at, 32), lo:hi] += g * scale


def bounded_kernel(
    lengths, weights, tq, tk, tv, sq, sk, sv, loss, top, oq, ok, ov,
    kv, rkv, rq, gq, gkv, rgkv, mine, theirs, t_sem, own_sem, send_sem, recv_sem, top_send, top_recv,
    ta, sb, bt, grad, lt, rt, ls, rs, et, es, diff, row_t, row_s, col, rvec, rb_t, rb_s, both, kl, log_sum,
):
    owner, me = lax.axis_index("dp"), lax.axis_index("tensor")
    length, weight = lengths[owner], weights[owner]
    valid = lax.broadcasted_iota(jnp.int32, (N, 1), 0) < length
    teacher = [
        pltpu.make_async_copy(tq.at[0], ta.at[:, pl.ds(0, 1024)], t_sem.at[0]),
        pltpu.make_async_copy(tk.at[0], ta.at[:, pl.ds(1024, 128)], t_sem.at[1]),
        pltpu.make_async_copy(tv.at[0], ta.at[:, pl.ds(1152, 128)], t_sem.at[2]),
    ]
    for c in teacher:
        c.start()
    for t in range(TS):
        kv[t] = fold_kv(sk[0, :, t * 32 : t * 32 + 32], sv[0, :, t * 32 : t * 32 + 32])

    barrier = pltpu.get_barrier_semaphore()
    for s in range(1, TS):
        pl.semaphore_signal(
            barrier, inc=1, device_id={"tensor": lax.rem(me + s, TS)}, device_id_type=MESH
        )
    def across(place, bit):
        return place + bit - 2 * bit * lax.rem(place // bit, 2)

    partners = [{"tensor": across(me, b)} for b in (1, 2, 4)]
    partners += [{"dp": across(owner, b)} for b in (1, 2, 4, 8, 16)]
    for p in partners[3:]:
        pl.semaphore_signal(barrier, inc=1, device_id=p, device_id_type=MESH)
    pl.semaphore_wait(barrier, TS - 1 + len(partners) - 3)

    def bounds(k):
        return pltpu.make_async_remote_copy(
            src_ref=mine.at[k],
            dst_ref=theirs.at[k],
            send_sem=top_send.at[k],
            recv_sem=top_recv.at[k],
            device_id=partners[k],
            device_id_type=MESH,
        )

    def at_rows(t):
        return pl.ds(pl.multiple_of(t * ROWS, ROWS), ROWS)

    def at_lanes(t, g=0, width=256):
        return pl.ds(pl.multiple_of(t * 256 + g * 128, 128), width)

    def ends(k, t):
        return (
            lambda: (kv.at[t], rkv.at[me]),
            lambda: (sq.at[0, :, at_lanes(t)], rq.at[at_rows(me), :]),
            lambda: (gq.at[0, at_rows(t), :], oq.at[0, :, at_lanes(me, 0, 128)]),
            lambda: (gq.at[1, at_rows(t), :], oq.at[0, :, at_lanes(me, 1, 128)]),
            lambda: (gkv.at[t], rgkv.at[me]),
        )[k]()

    def remote(k, s):
        peer = lax.rem(me + s, TS)
        src, dst = ends(k, peer)
        return pltpu.make_async_remote_copy(
            src_ref=src,
            dst_ref=dst,
            send_sem=send_sem.at[k, s],
            recv_sem=recv_sem.at[k, s],
            device_id={"tensor": peer},
            device_id_type=MESH,
        )

    def own(k):
        return pltpu.make_async_copy(*ends(k, me), own_sem.at[k])

    def start(k):
        for s in range(1, TS):
            remote(k, s).start()
        own(k).start()

    def arrived(k):
        own(k).wait()
        for s in range(1, TS):
            remote(k, s).wait_recv()

    def sent(k):
        for s in range(1, TS):
            remote(k, s).wait_send()

    start(0)
    start(1)
    grad[...] = jnp.zeros_like(grad)
    kl[...] = jnp.zeros_like(kl)
    log_sum[...] = jnp.zeros_like(log_sum)
    for c in teacher:
        c.wait()
    set_teacher(valid, ta, lt)
    arrived(0)
    set_student_kv(valid, rkv, sb, bt, ls)

    def leave(g):
        x = grad[128 * g : 128 * g + 128].T
        gq[g] = jnp.where(valid, x, 0.0).astype(bf16)
        start(2 + g)

    def step(n, carry):
        @pl.when(n == HEADS)
        def _():
            arrived(1)
            set_student_q(valid, rq, sb, bt, ls)
            mine[0] = jnp.maximum(
                jnp.maximum(bound_lanes(ta[:, 0:1024], 128), bound_lanes(ta[:, 1024:1280], 16)),
                jnp.maximum(bound_lanes(sb[:, 0:256], 32), bound_lanes(sb[:, 256:512], 4)),
            )
            bounds(0).start()

        for k in range(1, len(partners)):

            @pl.when(n == HEADS + k)
            def _():
                bounds(k - 1).wait()
                mine[k] = jnp.maximum(mine[k - 1], theirs[k - 1])
                bounds(k).start()

        @pl.when(n == HEADS + 4)
        def _():
            leave(0)

        @pl.when(n == HEADS + 8)
        def _():
            leave(1)

        one_head(n, length, weight, ta, sb, bt, grad, lt, rt, ls, rs, et, es, diff, row_t, row_s, col, rvec, rb_t, rb_s, both, kl, log_sum)
        return carry

    lax.fori_loop(0, 3 * HEADS, step, 0)
    x = jnp.concatenate([grad[256:320], jnp.zeros((64, N), f32)], axis=0).T
    x = jnp.where(valid, x, 0.0).astype(bf16).reshape(TS, 2, HALF, 128)
    gkv[...] = jnp.concatenate([x[:, 0, :, 0:64], x[:, 1, :, 0:64]], axis=2)
    start(4)
    total = (jnp.sum(kl[...]) + jnp.sum(log_sum[...])) * math.log(2.0)
    loss[0, 0] = total / length.astype(f32)
    last = len(partners) - 1
    bounds(last).wait()
    top[0, 0] = jnp.max(jnp.maximum(mine[last], theirs[last]))
    for k in range(2, 5):
        arrived(k)
    for i, out in enumerate((ok, ov)):
        for half in range(2):
            lo = half * 64 + i * 32
            out[0, half * HALF : half * HALF + HALF, :] = jnp.concatenate(
                [rgkv[t][:, lo : lo + 32] for t in range(TS)], axis=1
            )
    for k in range(5):
        sent(k)


def bounded_program(tq, tk, tv, sq, sk, sv, lengths, weights):
    smem = pl.BlockSpec(memory_space=pltpu.SMEM)
    vmem = pl.BlockSpec(memory_space=pltpu.VMEM)
    hbm = pl.BlockSpec(memory_space=pl.ANY)
    square = (N, N)
    message = (TS, HALF, 128)
    return pl.pallas_call(
        bounded_kernel,
        out_shape=(
            jax.ShapeDtypeStruct((1, 1), f32),
            jax.ShapeDtypeStruct((1, 1), f32),
            jax.ShapeDtypeStruct((1, ROWS, 2048), bf16),
            jax.ShapeDtypeStruct((1, ROWS, 256), bf16),
            jax.ShapeDtypeStruct((1, ROWS, 256), bf16),
        ),
        in_specs=[smem, smem, hbm, hbm, hbm, hbm, vmem, vmem],
        out_specs=[smem, smem, hbm, vmem, vmem],
        scratch_shapes=[
            pltpu.VMEM(message, bf16),
            pltpu.VMEM(message, bf16),
            pltpu.VMEM((N, 256), bf16),
            pltpu.VMEM((2, N, 128), bf16),
            pltpu.VMEM(message, bf16),
            pltpu.VMEM(message, bf16),
            pltpu.VMEM((8, 8, 128), f32),
            pltpu.VMEM((8, 8, 128), f32),
            pltpu.SemaphoreType.DMA((3,)),
            pltpu.SemaphoreType.DMA((5,)),
            pltpu.SemaphoreType.DMA((5, TS)),
            pltpu.SemaphoreType.DMA((5, TS)),
            pltpu.SemaphoreType.DMA((8,)),
            pltpu.SemaphoreType.DMA((8,)),
            pltpu.VMEM((N, 1280), bf16),
            pltpu.VMEM((N, 512), bf16),
            pltpu.VMEM((320, N), bf16),
            pltpu.VMEM((320, N), f32),
            pltpu.VMEM((N, 2560), bf16),
            pltpu.VMEM((N, 128), bf16),
            pltpu.VMEM((N, 1024), bf16),
            pltpu.VMEM((N, 128), bf16),
            pltpu.VMEM(square, f32),
            pltpu.VMEM(square, f32),
            pltpu.VMEM(square, f32),
            pltpu.VMEM((N, 128), f32),
            pltpu.VMEM((N, 128), f32),
            pltpu.VMEM((16, N), f32),
            pltpu.VMEM((16, N), f32),
            pltpu.VMEM((N, 128), f32),
            pltpu.VMEM((N, 128), f32),
            pltpu.VMEM(square, bf16),
            pltpu.VMEM((8, N), f32),
            pltpu.VMEM((8, N), f32),
        ],
        compiler_params=pltpu.CompilerParams(
            collective_id=0, has_side_effects=True, vmem_limit_bytes=VMEM_LIMIT
        ),
        cost_estimate=pl.CostEstimate(
            flops=40 * 10**9, bytes_accessed=4 * 10**6, transcendentals=32 * 10**6
        ),
    )(lengths, weights, tq, tk, tv, sq, sk, sv)


def keep_kernel(loss, q, k, v, loss_out, q_out, k_out, v_out):
    loss_out[0, 0] = loss[0, 0]
    q_out[...], k_out[...], v_out[...] = q[...], k[...], v[...]


def keep(*results):
    smem = pl.BlockSpec(memory_space=pltpu.SMEM)
    specs = [smem] + [pl.BlockSpec(memory_space=pltpu.VMEM)] * 3
    return pl.pallas_call(
        keep_kernel,
        out_shape=[jax.ShapeDtypeStruct(r.shape, r.dtype) for r in results],
        in_specs=specs,
        out_specs=specs,
    )(*results)


def on_device(*arrays):
    loss, bound, *gradients = bounded_program(*arrays)
    return lax.cond(
        bound[0, 0] <= SAFE_LOG2,
        lambda: tuple(keep(loss, *gradients)),
        lambda: general_program(*arrays),
    )


def solution(mesh):
    in_specs = (
        P("dp", None, "tensor"),
        P("dp", None, "tensor"),
        P("dp", None, "tensor"),
        P("dp", "tensor", None),
        P("dp", "tensor", None),
        P("dp", "tensor", None),
        P(),
        P(),
    )
    out_specs = (
        P("dp", "tensor"),
        P("dp", "tensor", None),
        P("dp", "tensor", None),
        P("dp", "tensor", None),
    )
    return jax.shard_map(
        on_device, mesh=mesh, in_specs=in_specs, out_specs=out_specs, check_vma=False
    )
```

```python
import functools
import math

import jax
import jax.numpy as jnp
from jax import lax
from jax.experimental import pallas as pl
from jax.experimental.pallas import tpu as pltpu
from jax.sharding import PartitionSpec as P

bf16, f32 = jnp.bfloat16, jnp.float32
MESH = pl.DeviceIdType.MESH
NT = (((1,), (1,)), ((), ()))
NN = (((1,), (0,)), ((), ()))
N = 1024
TS = 8
ROWS = N // TS
HALF = ROWS // 2
HEADS = 8
BL = 256
NB = N // BL
LOG2E = math.log2(math.e)
SAFE_LOG2 = 115.0
VMEM_LIMIT = 60 * 2**20


RELATION_COUNT = 64


def as_sent(value):
    return jax.tree.map(lambda a: a.astype(jnp.bfloat16) if a.dtype == jnp.float32 else a, value)


def head_terms(teach, stud, length, weight):
    seq_len = teach.shape[0]
    block_rows = min(512, seq_len)
    teach_scale = teach.shape[1] ** (-0.5)
    stud_scale = stud.shape[1] ** (-0.5)
    key_positions = jnp.arange(seq_len, dtype=jnp.int32)
    valid_keys = key_positions[None, :] < length
    kl_total = jnp.zeros((), jnp.float32)
    across = jnp.zeros(stud.shape, jnp.float32)
    row_parts = []
    for row_start in range(0, seq_len, block_rows):
        teach_rows = teach[row_start : row_start + block_rows]
        stud_rows = stud[row_start : row_start + block_rows]
        teach_score = jnp.dot(teach_rows, teach.T, preferred_element_type=jnp.float32) * teach_scale
        stud_score = jnp.dot(stud_rows, stud.T, preferred_element_type=jnp.float32) * stud_scale
        teach_score = jnp.where(valid_keys, teach_score, -1e30)
        stud_score = jnp.where(valid_keys, stud_score, -1e30)
        log_teach = jax.nn.log_softmax(teach_score, axis=1)
        log_stud = jax.nn.log_softmax(stud_score, axis=1)
        prob_teach = jnp.exp(log_teach)
        prob_stud = jnp.exp(log_stud)
        valid_rows = row_start + jnp.arange(block_rows, dtype=jnp.int32) < length
        row_divergence = jnp.sum(
            jnp.where(valid_keys, prob_teach * (log_teach - log_stud), 0.0), axis=1
        )
        kl_total = kl_total + jnp.sum(jnp.where(valid_rows, row_divergence, 0.0))
        slope_rows = jnp.where(valid_rows[:, None], weight * (prob_stud - prob_teach), 0.0).astype(
            jnp.bfloat16
        )
        row_parts.append(jnp.dot(slope_rows, stud, preferred_element_type=jnp.float32))
        across = across + lax.dot_general(
            slope_rows, stud_rows, (((0,), (0,)), ((), ())), preferred_element_type=jnp.float32
        )
    gradient = ((jnp.concatenate(row_parts, axis=0) + across) * stud_scale).astype(jnp.bfloat16)
    return (kl_total, gradient)


def kind_pass(teach_heads, stud_heads, length, weight):

    def one_head(head_pair):
        return head_terms(head_pair[0], head_pair[1], length, weight)

    head_losses, gradients = lax.map(one_head, (teach_heads, stud_heads))
    return (jnp.sum(head_losses), gradients)


def split_heads(values, head_count):
    return values.reshape(values.shape[0], head_count, values.shape[1] // head_count).transpose(
        1, 0, 2
    )


def general_program(
    teacher_q, teacher_k, teacher_v, student_q, student_k, student_v, lengths, seq_weight
):
    tensor_size = lax.axis_size("tensor")
    head_count = RELATION_COUNT // tensor_size
    owner_index = lax.axis_index("dp")
    length = lax.dynamic_index_in_dim(lengths, owner_index, 0, keepdims=False)
    weight = lax.dynamic_index_in_dim(seq_weight, owner_index, 0, keepdims=False)
    seq_len = teacher_q.shape[1]

    def spread(values):
        return values.reshape(
            values.shape[0], values.shape[1], tensor_size, values.shape[2] // tensor_size
        )

    def settle(values):
        return split_heads(values.reshape(seq_len, values.shape[3]), head_count)

    def gather_back(gradients):
        return gradients.transpose(1, 0, 2).reshape(1, seq_len, 1, -1)

    def restore(values):
        return values.reshape(values.shape[0], values.shape[1], values.shape[2] * values.shape[3])

    teach_queries = split_heads(teacher_q[0], head_count)
    teach_keys = split_heads(teacher_k[0], head_count)
    teach_values = split_heads(teacher_v[0], head_count)
    got_queries, got_keys, got_values = (
        lax.all_to_all(spread(student_q), "tensor", split_axis=2, concat_axis=1, tiled=True),
        lax.all_to_all(spread(student_k), "tensor", split_axis=2, concat_axis=1, tiled=True),
        lax.all_to_all(spread(student_v), "tensor", split_axis=2, concat_axis=1, tiled=True),
    )
    query_loss, query_grads = kind_pass(teach_queries, settle(got_queries), length, weight)
    key_loss, key_grads = kind_pass(teach_keys, settle(got_keys), length, weight)
    value_loss, value_grads = kind_pass(teach_values, settle(got_values), length, weight)
    query_back, key_back, value_back = (
        lax.all_to_all(
            as_sent(gather_back(query_grads)), "tensor", split_axis=1, concat_axis=2, tiled=True
        ),
        lax.all_to_all(
            as_sent(gather_back(key_grads)), "tensor", split_axis=1, concat_axis=2, tiled=True
        ),
        lax.all_to_all(
            as_sent(gather_back(value_grads)), "tensor", split_axis=1, concat_axis=2, tiled=True
        ),
    )
    kl_sum = query_loss + key_loss + value_loss
    relation_loss = (kl_sum / length.astype(jnp.float32)).reshape(1, 1)
    return (relation_loss, restore(query_back), restore(key_back), restore(value_back))


def bound_lanes(x, w):
    top = jnp.max(jnp.abs(x).astype(f32).reshape(N // 8, 8, x.shape[1]), axis=0)
    top = functools.reduce(jnp.maximum, [top[:, c : c + 128] for c in range(0, x.shape[1], 128)])
    return (LOG2E * 1.0001 * w**0.5) * top * top


def dot(a, b, dims):
    return lax.dot_general(a, b, dims, preferred_element_type=f32)


def fold_kv(k, v):
    return jnp.concatenate([k[:HALF], v[:HALF], k[HALF:], v[HALF:]], axis=1)


class Head:
    def __init__(self, n):
        q = (n >= HEADS) & (n < 2 * HEADS)
        kv = jnp.where(n < HEADS, 0, 1)
        sub = lax.rem(n, HEADS)
        self.t_group = jnp.where(q, sub, HEADS + kv)
        self.s_group = jnp.where(q, sub // 4, 2 + kv)
        self.t_at = pl.multiple_of(self.t_group * 128, 128)
        self.s_at = pl.multiple_of(self.s_group * 128, 128)
        self.g_at = pl.multiple_of(jnp.where(q, 32 * sub, 256 + 32 * kv), 32)
        self.t_scale = jnp.where(q, LOG2E * 128**-0.5, LOG2E * 0.25).astype(f32)
        self.s_scale = jnp.where(q, LOG2E * 32**-0.5, LOG2E * 0.5).astype(f32)
        self.g_scale = jnp.where(q, 32**-0.5, 0.5).astype(f32)
        self.t_lo = jnp.where(q, 0, 16 * sub)
        self.t_hi = jnp.where(q, 128, 16 * sub + 16)
        self.s_lo = jnp.where(q, 32 * lax.rem(sub, 4), 4 * sub)
        self.s_hi = self.s_lo + jnp.where(q, 32, 4)
        self.b_lo = jnp.where(q, 0, 4 * sub)
        self.b_hi = jnp.where(q, 32, 4 * sub + 4)


def split_scaled(x, scale, left, at):
    y = x.astype(f32) * scale
    top = y.astype(bf16)
    left[at, :, 0:128] = top
    left[at, :, 128:256] = (y - top.astype(f32)).astype(bf16)


def set_teacher(valid, ta, lt):
    for g in range(HEADS + 2):
        at = g * 128
        x = jnp.where(valid, ta[:, at : at + 128].astype(f32), 0.0).astype(bf16)
        ta[:, at : at + 128] = x
        split_scaled(x, LOG2E * (128**-0.5 if g < HEADS else 0.25), lt, g)


def set_student_kv(valid, rkv, sb, bt, ls):
    folded = rkv[...]
    for i in range(2):
        halves = [folded[:, :, 64 * h + 32 * i : 64 * h + 32 * i + 32] for h in range(2)]
        b = jnp.concatenate(halves, axis=1).reshape(N, 32)
        b = jnp.where(valid, jnp.concatenate([b, jnp.zeros((N, 96), bf16)], axis=1).astype(f32), 0.0)
        at = 256 + 128 * i
        sb[:, at : at + 128] = b.astype(bf16)
        bt[256 + 32 * i : 288 + 32 * i] = b.T[0:32].astype(bf16)
        split_scaled(b.astype(bf16), LOG2E * 0.5, ls, 2 + i)


def set_student_q(valid, rq, sb, bt, ls):
    for g in range(2):
        at = 128 * g
        b = jnp.where(valid, rq[:, at : at + 128].astype(f32), 0.0)
        sb[:, at : at + 128] = b.astype(bf16)
        bt[at : at + 128] = b.T.astype(bf16)
        split_scaled(b.astype(bf16), LOG2E * 32**-0.5, ls, g)


def right_operands(h, ta, sb, rt, rs):
    lane = lax.broadcasted_iota(jnp.int32, (1, 128), 1)

    def keep(lo, hi):
        return ((lane >= lo) & (lane < hi)).astype(f32).astype(bf16)

    rt[...] = ta[:, pl.ds(h.t_at, 128)] * keep(h.t_lo, h.t_hi)
    rs[...] = sb[:, pl.ds(h.s_at, 128)] * keep(h.s_lo, h.s_hi)


def head_columns(h, bt):
    sub = lax.broadcasted_iota(jnp.int32, (32, 1), 0)
    b = bt[pl.ds(h.g_at, 32), :].astype(f32)
    return jnp.where((sub >= h.b_lo) & (sub < h.b_hi), b, 0.0).astype(bf16)


def folded_sum(x):
    return x.reshape(x.shape[0] // 8, 8, x.shape[1]).sum(0)


def first_block(i, j, h, lt, rt, ls, rs, et, es, diff, row_t, row_s, col):
    ri, rj = pl.ds(i * BL, BL), pl.ds(j * BL, BL)
    x_t = dot(lt[h.t_group, ri], jnp.concatenate([rt[rj], rt[rj]], axis=1), NT)
    x_s = dot(ls[h.s_group, ri], jnp.concatenate([rs[rj], rs[rj]], axis=1), NT)
    e_t, e_s = jnp.exp2(x_t), jnp.exp2(x_s)
    et[ri, rj] = e_t
    es[ri, rj] = e_s
    diff[ri, rj] = x_t - x_s
    if i == 0:
        col[0:8, rj] = folded_sum(e_t)
        col[8:16, rj] = folded_sum(e_s)
    else:
        col[0:8, rj] += folded_sum(e_t)
        col[8:16, rj] += folded_sum(e_s)
    if j == i + 1:
        row_t[ri] = e_t[:, :128] + e_t[:, 128:]
        row_s[ri] = e_s[:, :128] + e_s[:, 128:]
    elif j > i:
        row_t[ri] += e_t[:, :128] + e_t[:, 128:]
        row_s[ri] += e_s[:, :128] + e_s[:, 128:]


def row_statistics(length, row_t, row_s, col, rvec, rb_t, rb_s, log_sum):
    valid = lax.broadcasted_iota(jnp.int32, (1, N), 1) < length
    padded = (N - length).astype(f32)

    def total(row, c):
        r = jnp.sum(row[0 : N - BL].T, axis=0, keepdims=True)
        r = jnp.concatenate([r, jnp.zeros((1, BL), f32)], axis=1)
        return jnp.where(valid, r + jnp.sum(c, axis=0, keepdims=True) - padded, 1.0)

    sum_t, sum_s = total(row_t, col[0:8]), total(row_s, col[8:16])
    r_t, r_s = jnp.where(valid, 1.0 / sum_t, 0.0), jnp.where(valid, 1.0 / sum_s, 0.0)
    rvec[0:8] = jnp.broadcast_to(r_t, (8, N))
    rvec[8:16] = jnp.broadcast_to(r_s, (8, N))
    rb_t[...] = jnp.broadcast_to(r_t, (128, N)).T
    rb_s[...] = jnp.broadcast_to(r_s, (128, N)).T
    log_sum[0:1, :] += jnp.log2(sum_s) - jnp.log2(sum_t)


def second_block(i, j, et, es, diff, rvec, rb_t, rb_s, both, kl):
    ri, rj = pl.ds(i * BL, BL), pl.ds(j * BL, BL)

    def pair(by_row, by_col):
        wide = jnp.concatenate([by_row, by_row], axis=1).reshape(BL // 8, 8, BL)
        return (wide + by_col[None]).reshape(BL, BL)

    q_t = et[ri, rj] * pair(rb_t[ri], rvec[0:8, rj])
    both[ri, rj] = (es[ri, rj] * pair(rb_s[ri], rvec[8:16, rj]) - q_t).astype(bf16)
    part = folded_sum(q_t * diff[ri, rj])
    kl[:, rj] += 0.5 * part if i == j else part


def gradient(n, weight, bt, grad, both):
    h = Head(n)
    b = head_columns(h, bt)
    scale = h.g_scale * weight
    for j in range(NB):
        lo, hi = j * BL, (j + 1) * BL
        g = dot(b[:, :hi], both[0:hi, lo:hi], NN)
        if hi < N:
            g = g + dot(b[:, hi:], both[lo:hi, hi:N], NT)
        grad[pl.ds(h.g_at, 32), lo:hi] += g * scale


def one_head(n, length, weight, ta, sb, bt, grad, lt, rt, ls, rs, et, es, diff, row_t, row_s, col, rvec, rb_t, rb_s, both, kl, log_sum):
    h = Head(n)
    right_operands(h, ta, sb, rt, rs)
    for j in range(NB):
        for i in range(j + 1):
            first_block(i, j, h, lt, rt, ls, rs, et, es, diff, row_t, row_s, col)
    row_statistics(length, row_t, row_s, col, rvec, rb_t, rb_s, log_sum)
    gradient(jnp.maximum(n - 1, 0), weight, bt, grad, both)
    for j in range(NB):
        for i in range(j + 1):
            second_block(i, j, et, es, diff, rvec, rb_t, rb_s, both, kl)


def bounded_kernel(
    lengths, weights, tq, tk, tv, sq, sk, sv, loss, top, oq, ok, ov,
    kv, rkv, rq, gq, gkv, rgkv, mine, theirs, t_sem, own_sem, send_sem, recv_sem,
    ta, sb, bt, grad, lt, rt, ls, rs, et, es, diff, row_t, row_s, col, rvec, rb_t, rb_s, both, kl, log_sum,
):
    owner, me = lax.axis_index("dp"), lax.axis_index("tensor")
    length, weight = lengths[owner], weights[owner]
    valid = lax.broadcasted_iota(jnp.int32, (N, 1), 0) < length
    teacher = [
        pltpu.make_async_copy(tq.at[0], ta.at[:, pl.ds(0, 1024)], t_sem.at[0]),
        pltpu.make_async_copy(tk.at[0], ta.at[:, pl.ds(1024, 128)], t_sem.at[1]),
        pltpu.make_async_copy(tv.at[0], ta.at[:, pl.ds(1152, 128)], t_sem.at[2]),
    ]
    for c in teacher:
        c.start()
    for t in range(TS):
        kv[t] = fold_kv(sk[0, :, t * 32 : t * 32 + 32], sv[0, :, t * 32 : t * 32 + 32])

    barrier = pltpu.get_barrier_semaphore()
    for s in range(1, TS):
        pl.semaphore_signal(
            barrier, inc=1, device_id={"tensor": lax.rem(me + s, TS)}, device_id_type=MESH
        )
    pl.semaphore_wait(barrier, TS - 1)

    def at_rows(t):
        return pl.ds(pl.multiple_of(t * ROWS, ROWS), ROWS)

    def at_lanes(t, g=0, width=256):
        return pl.ds(pl.multiple_of(t * 256 + g * 128, 128), width)

    def ends(k, t):
        return (
            lambda: (kv.at[t], rkv.at[me]),
            lambda: (sq.at[0, :, at_lanes(t)], rq.at[at_rows(me), :]),
            lambda: (gq.at[0, at_rows(t), :], oq.at[0, :, at_lanes(me, 0, 128)]),
            lambda: (gq.at[1, at_rows(t), :], oq.at[0, :, at_lanes(me, 1, 128)]),
            lambda: (gkv.at[t], rgkv.at[me]),
            lambda: (mine, theirs.at[me]),
        )[k]()

    def remote(k, s):
        peer = lax.rem(me + s, TS)
        src, dst = ends(k, peer)
        return pltpu.make_async_remote_copy(
            src_ref=src,
            dst_ref=dst,
            send_sem=send_sem.at[k, s],
            recv_sem=recv_sem.at[k, s],
            device_id={"tensor": peer},
            device_id_type=MESH,
        )

    def own(k):
        return pltpu.make_async_copy(*ends(k, me), own_sem.at[k])

    def start(k):
        for s in range(1, TS):
            remote(k, s).start()
        own(k).start()

    def arrived(k):
        own(k).wait()
        for s in range(1, TS):
            remote(k, s).wait_recv()

    def sent(k):
        for s in range(1, TS):
            remote(k, s).wait_send()

    start(0)
    grad[...] = jnp.zeros_like(grad)
    kl[...] = jnp.zeros_like(kl)
    log_sum[...] = jnp.zeros_like(log_sum)
    both[...] = jnp.zeros_like(both)
    for c in teacher:
        c.wait()
    set_teacher(valid, ta, lt)
    arrived(0)
    start(1)
    set_student_kv(valid, rkv, sb, bt, ls)

    def leave(g):
        x = grad[128 * g : 128 * g + 128].T
        gq[g] = jnp.where(valid, x, 0.0).astype(bf16)
        start(2 + g)

    def step(n, carry):
        @pl.when(n == HEADS)
        def _():
            arrived(1)
            set_student_q(valid, rq, sb, bt, ls)
            mine[...] = jnp.maximum(
                jnp.maximum(bound_lanes(ta[:, 0:1024], 128), bound_lanes(ta[:, 1024:1280], 16)),
                jnp.maximum(bound_lanes(sb[:, 0:256], 32), bound_lanes(sb[:, 256:512], 4)),
            )
            start(5)

        @pl.when(n == HEADS + 5)
        def _():
            leave(0)

        @pl.when(n == HEADS + 9)
        def _():
            leave(1)

        one_head(n, length, weight, ta, sb, bt, grad, lt, rt, ls, rs, et, es, diff, row_t, row_s, col, rvec, rb_t, rb_s, both, kl, log_sum)
        return carry

    lax.fori_loop(0, 3 * HEADS, step, 0)
    gradient(3 * HEADS - 1, weight, bt, grad, both)
    x = jnp.concatenate([grad[256:320], jnp.zeros((64, N), f32)], axis=0).T
    x = jnp.where(valid, x, 0.0).astype(bf16).reshape(TS, 2, HALF, 128)
    gkv[...] = jnp.concatenate([x[:, 0, :, 0:64], x[:, 1, :, 0:64]], axis=2)
    start(4)
    total = (jnp.sum(kl[...]) + jnp.sum(log_sum[...])) * math.log(2.0)
    loss[0, 0] = total / length.astype(f32)
    arrived(5)
    top[0, 0] = jnp.max(theirs[...])
    for k in range(2, 5):
        arrived(k)
    for i, out in enumerate((ok, ov)):
        for half in range(2):
            lo = half * 64 + i * 32
            out[0, half * HALF : half * HALF + HALF, :] = jnp.concatenate(
                [rgkv[t][:, lo : lo + 32] for t in range(TS)], axis=1
            )
    for k in range(6):
        sent(k)


def bounded_program(tq, tk, tv, sq, sk, sv, lengths, weights):
    smem = pl.BlockSpec(memory_space=pltpu.SMEM)
    vmem = pl.BlockSpec(memory_space=pltpu.VMEM)
    hbm = pl.BlockSpec(memory_space=pl.ANY)
    square = (N, N)
    message = (TS, HALF, 128)
    return pl.pallas_call(
        bounded_kernel,
        out_shape=(
            jax.ShapeDtypeStruct((1, 1), f32),
            jax.ShapeDtypeStruct((1, 1), f32),
            jax.ShapeDtypeStruct((1, ROWS, 2048), bf16),
            jax.ShapeDtypeStruct((1, ROWS, 256), bf16),
            jax.ShapeDtypeStruct((1, ROWS, 256), bf16),
        ),
        in_specs=[smem, smem, hbm, hbm, hbm, hbm, vmem, vmem],
        out_specs=[smem, smem, hbm, vmem, vmem],
        scratch_shapes=[
            pltpu.VMEM(message, bf16),
            pltpu.VMEM(message, bf16),
            pltpu.VMEM((N, 256), bf16),
            pltpu.VMEM((2, N, 128), bf16),
            pltpu.VMEM(message, bf16),
            pltpu.VMEM(message, bf16),
            pltpu.VMEM((8, 128), f32),
            pltpu.VMEM((TS, 8, 128), f32),
            pltpu.SemaphoreType.DMA((3,)),
            pltpu.SemaphoreType.DMA((6,)),
            pltpu.SemaphoreType.DMA((6, TS)),
            pltpu.SemaphoreType.DMA((6, TS)),
            pltpu.VMEM((N, 1280), bf16),
            pltpu.VMEM((N, 512), bf16),
            pltpu.VMEM((320, N), bf16),
            pltpu.VMEM((320, N), f32),
            pltpu.VMEM((HEADS + 2, N, 256), bf16),
            pltpu.VMEM((N, 128), bf16),
            pltpu.VMEM((4, N, 256), bf16),
            pltpu.VMEM((N, 128), bf16),
            pltpu.VMEM(square, f32),
            pltpu.VMEM(square, f32),
            pltpu.VMEM(square, f32),
            pltpu.VMEM((N, 128), f32),
            pltpu.VMEM((N, 128), f32),
            pltpu.VMEM((16, N), f32),
            pltpu.VMEM((16, N), f32),
            pltpu.VMEM((N, 128), f32),
            pltpu.VMEM((N, 128), f32),
            pltpu.VMEM(square, bf16),
            pltpu.VMEM((8, N), f32),
            pltpu.VMEM((8, N), f32),
        ],
        compiler_params=pltpu.CompilerParams(
            collective_id=0, has_side_effects=True, vmem_limit_bytes=VMEM_LIMIT
        ),
        cost_estimate=pl.CostEstimate(
            flops=40 * 10**9, bytes_accessed=4 * 10**6, transcendentals=32 * 10**6
        ),
    )(lengths, weights, tq, tk, tv, sq, sk, sv)


def keep_kernel(loss, q, k, v, loss_out, q_out, k_out, v_out):
    loss_out[0, 0] = loss[0, 0]
    q_out[...], k_out[...], v_out[...] = q[...], k[...], v[...]


def keep(*results):
    smem = pl.BlockSpec(memory_space=pltpu.SMEM)
    specs = [smem] + [pl.BlockSpec(memory_space=pltpu.VMEM)] * 3
    return pl.pallas_call(
        keep_kernel,
        out_shape=[jax.ShapeDtypeStruct(r.shape, r.dtype) for r in results],
        in_specs=specs,
        out_specs=specs,
    )(*results)


def on_device(*arrays):
    loss, bound, *gradients = bounded_program(*arrays)
    return lax.cond(
        bound[0, 0] <= SAFE_LOG2,
        lambda: tuple(keep(loss, *gradients)),
        lambda: general_program(*arrays),
    )


def solution(mesh):
    in_specs = (
        P("dp", None, "tensor"),
        P("dp", None, "tensor"),
        P("dp", None, "tensor"),
        P("dp", "tensor", None),
        P("dp", "tensor", None),
        P("dp", "tensor", None),
        P(),
        P(),
    )
    out_specs = (
        P("dp", "tensor"),
        P("dp", "tensor", None),
        P("dp", "tensor", None),
        P("dp", "tensor", None),
    )
    return jax.shard_map(
        on_device, mesh=mesh, in_specs=in_specs, out_specs=out_specs, check_vma=False
    )
```

```python
import functools
import math

import jax
import jax.numpy as jnp
from jax import lax
from jax.experimental import pallas as pl
from jax.experimental.pallas import tpu as pltpu
from jax.sharding import PartitionSpec as P

bf16, f32 = jnp.bfloat16, jnp.float32
MESH = pl.DeviceIdType.MESH
NT = (((1,), (1,)), ((), ()))
NN = (((1,), (0,)), ((), ()))
N = 1024
TS = 8
ROWS = N // TS
HALF = ROWS // 2
HEADS = 8
BL = 256
NB = N // BL
LOG2E = math.log2(math.e)
SAFE_LOG2 = 115.0
VMEM_LIMIT = 60 * 2**20


RELATION_COUNT = 64


def as_sent(value):
    return jax.tree.map(lambda a: a.astype(jnp.bfloat16) if a.dtype == jnp.float32 else a, value)


def head_terms(teach, stud, length, weight):
    seq_len = teach.shape[0]
    block_rows = min(512, seq_len)
    teach_scale = teach.shape[1] ** (-0.5)
    stud_scale = stud.shape[1] ** (-0.5)
    key_positions = jnp.arange(seq_len, dtype=jnp.int32)
    valid_keys = key_positions[None, :] < length
    kl_total = jnp.zeros((), jnp.float32)
    across = jnp.zeros(stud.shape, jnp.float32)
    row_parts = []
    for row_start in range(0, seq_len, block_rows):
        teach_rows = teach[row_start : row_start + block_rows]
        stud_rows = stud[row_start : row_start + block_rows]
        teach_score = jnp.dot(teach_rows, teach.T, preferred_element_type=jnp.float32) * teach_scale
        stud_score = jnp.dot(stud_rows, stud.T, preferred_element_type=jnp.float32) * stud_scale
        teach_score = jnp.where(valid_keys, teach_score, -1e30)
        stud_score = jnp.where(valid_keys, stud_score, -1e30)
        log_teach = jax.nn.log_softmax(teach_score, axis=1)
        log_stud = jax.nn.log_softmax(stud_score, axis=1)
        prob_teach = jnp.exp(log_teach)
        prob_stud = jnp.exp(log_stud)
        valid_rows = row_start + jnp.arange(block_rows, dtype=jnp.int32) < length
        row_divergence = jnp.sum(
            jnp.where(valid_keys, prob_teach * (log_teach - log_stud), 0.0), axis=1
        )
        kl_total = kl_total + jnp.sum(jnp.where(valid_rows, row_divergence, 0.0))
        slope_rows = jnp.where(valid_rows[:, None], weight * (prob_stud - prob_teach), 0.0).astype(
            jnp.bfloat16
        )
        row_parts.append(jnp.dot(slope_rows, stud, preferred_element_type=jnp.float32))
        across = across + lax.dot_general(
            slope_rows, stud_rows, (((0,), (0,)), ((), ())), preferred_element_type=jnp.float32
        )
    gradient = ((jnp.concatenate(row_parts, axis=0) + across) * stud_scale).astype(jnp.bfloat16)
    return (kl_total, gradient)


def kind_pass(teach_heads, stud_heads, length, weight):

    def one_head(head_pair):
        return head_terms(head_pair[0], head_pair[1], length, weight)

    head_losses, gradients = lax.map(one_head, (teach_heads, stud_heads))
    return (jnp.sum(head_losses), gradients)


def split_heads(values, head_count):
    return values.reshape(values.shape[0], head_count, values.shape[1] // head_count).transpose(
        1, 0, 2
    )


def general_program(
    teacher_q, teacher_k, teacher_v, student_q, student_k, student_v, lengths, seq_weight
):
    tensor_size = lax.axis_size("tensor")
    head_count = RELATION_COUNT // tensor_size
    owner_index = lax.axis_index("dp")
    length = lax.dynamic_index_in_dim(lengths, owner_index, 0, keepdims=False)
    weight = lax.dynamic_index_in_dim(seq_weight, owner_index, 0, keepdims=False)
    seq_len = teacher_q.shape[1]

    def spread(values):
        return values.reshape(
            values.shape[0], values.shape[1], tensor_size, values.shape[2] // tensor_size
        )

    def settle(values):
        return split_heads(values.reshape(seq_len, values.shape[3]), head_count)

    def gather_back(gradients):
        return gradients.transpose(1, 0, 2).reshape(1, seq_len, 1, -1)

    def restore(values):
        return values.reshape(values.shape[0], values.shape[1], values.shape[2] * values.shape[3])

    teach_queries = split_heads(teacher_q[0], head_count)
    teach_keys = split_heads(teacher_k[0], head_count)
    teach_values = split_heads(teacher_v[0], head_count)
    got_queries, got_keys, got_values = (
        lax.all_to_all(spread(student_q), "tensor", split_axis=2, concat_axis=1, tiled=True),
        lax.all_to_all(spread(student_k), "tensor", split_axis=2, concat_axis=1, tiled=True),
        lax.all_to_all(spread(student_v), "tensor", split_axis=2, concat_axis=1, tiled=True),
    )
    query_loss, query_grads = kind_pass(teach_queries, settle(got_queries), length, weight)
    key_loss, key_grads = kind_pass(teach_keys, settle(got_keys), length, weight)
    value_loss, value_grads = kind_pass(teach_values, settle(got_values), length, weight)
    query_back, key_back, value_back = (
        lax.all_to_all(
            as_sent(gather_back(query_grads)), "tensor", split_axis=1, concat_axis=2, tiled=True
        ),
        lax.all_to_all(
            as_sent(gather_back(key_grads)), "tensor", split_axis=1, concat_axis=2, tiled=True
        ),
        lax.all_to_all(
            as_sent(gather_back(value_grads)), "tensor", split_axis=1, concat_axis=2, tiled=True
        ),
    )
    kl_sum = query_loss + key_loss + value_loss
    relation_loss = (kl_sum / length.astype(jnp.float32)).reshape(1, 1)
    return (relation_loss, restore(query_back), restore(key_back), restore(value_back))


def bound_lanes(x, w):
    top = jnp.max(jnp.abs(x).astype(f32).reshape(N // 8, 8, x.shape[1]), axis=0)
    top = functools.reduce(jnp.maximum, [top[:, c : c + 128] for c in range(0, x.shape[1], 128)])
    return (LOG2E * 1.0001 * w**0.5) * top * top


def dot(a, b, dims):
    return lax.dot_general(a, b, dims, preferred_element_type=f32)


def fold_kv(k, v):
    return jnp.concatenate([k[:HALF], v[:HALF], k[HALF:], v[HALF:]], axis=1)


class Head:
    def __init__(self, n):
        q = (n >= HEADS) & (n < 2 * HEADS)
        kv = jnp.where(n < HEADS, 0, 1)
        sub = lax.rem(n, HEADS)
        self.t_group = jnp.where(q, sub, HEADS + kv)
        self.s_group = jnp.where(q, sub // 4, 2 + kv)
        self.t_at = pl.multiple_of(self.t_group * 128, 128)
        self.s_at = pl.multiple_of(self.s_group * 128, 128)
        self.g_at = pl.multiple_of(jnp.where(q, 32 * sub, 256 + 32 * kv), 32)
        self.t_scale = jnp.where(q, LOG2E * 128**-0.5, LOG2E * 0.25).astype(f32)
        self.s_scale = jnp.where(q, LOG2E * 32**-0.5, LOG2E * 0.5).astype(f32)
        self.g_scale = jnp.where(q, 32**-0.5, 0.5).astype(f32)
        self.t_lo = jnp.where(q, 0, 16 * sub)
        self.t_hi = jnp.where(q, 128, 16 * sub + 16)
        self.s_lo = jnp.where(q, 32 * lax.rem(sub, 4), 4 * sub)
        self.s_hi = self.s_lo + jnp.where(q, 32, 4)
        self.b_lo = jnp.where(q, 0, 4 * sub)
        self.b_hi = jnp.where(q, 32, 4 * sub + 4)


def split_scaled(x, scale, left, at):
    y = x.astype(f32) * scale
    top = y.astype(bf16)
    left[at, :, 0:128] = top
    left[at, :, 128:256] = (y - top.astype(f32)).astype(bf16)


def set_teacher(valid, ta, lt):
    for g in range(HEADS + 2):
        at = g * 128
        x = jnp.where(valid, ta[:, at : at + 128].astype(f32), 0.0).astype(bf16)
        ta[:, at : at + 128] = x
        split_scaled(x, LOG2E * (128**-0.5 if g < HEADS else 0.25), lt, g)


def set_student_kv(valid, rkv, sb, bt, ls):
    folded = rkv[...]
    for i in range(2):
        halves = [folded[:, :, 64 * h + 32 * i : 64 * h + 32 * i + 32] for h in range(2)]
        b = jnp.concatenate(halves, axis=1).reshape(N, 32)
        b = jnp.where(valid, jnp.concatenate([b, jnp.zeros((N, 96), bf16)], axis=1).astype(f32), 0.0)
        at = 256 + 128 * i
        sb[:, at : at + 128] = b.astype(bf16)
        bt[256 + 32 * i : 288 + 32 * i] = b.T[0:32].astype(bf16)
        split_scaled(b.astype(bf16), LOG2E * 0.5, ls, 2 + i)


def set_student_q(valid, rq, sb, bt, ls):
    for g in range(2):
        at = 128 * g
        b = jnp.where(valid, rq[:, at : at + 128].astype(f32), 0.0)
        sb[:, at : at + 128] = b.astype(bf16)
        bt[at : at + 128] = b.T.astype(bf16)
        split_scaled(b.astype(bf16), LOG2E * 32**-0.5, ls, g)


def right_operands(h, ta, sb, rt, rs):
    lane = lax.broadcasted_iota(jnp.int32, (1, 128), 1)

    def keep(lo, hi):
        return ((lane >= lo) & (lane < hi)).astype(f32).astype(bf16)

    rt[...] = ta[:, pl.ds(h.t_at, 128)] * keep(h.t_lo, h.t_hi)
    rs[...] = sb[:, pl.ds(h.s_at, 128)] * keep(h.s_lo, h.s_hi)


def head_columns(h, bt):
    sub = lax.broadcasted_iota(jnp.int32, (32, 1), 0)
    b = bt[pl.ds(h.g_at, 32), :].astype(f32)
    return jnp.where((sub >= h.b_lo) & (sub < h.b_hi), b, 0.0).astype(bf16)


def folded_sum(x):
    return x.reshape(x.shape[0] // 8, 8, x.shape[1]).sum(0)


def first_block(i, j, h, lt, rt, ls, rs, et, es, diff, row_t, row_s, col):
    ri, rj = pl.ds(i * BL, BL), pl.ds(j * BL, BL)
    x_t = dot(lt[h.t_group, ri], jnp.concatenate([rt[rj], rt[rj]], axis=1), NT)
    x_s = dot(ls[h.s_group, ri], jnp.concatenate([rs[rj], rs[rj]], axis=1), NT)
    e_t, e_s = jnp.exp2(x_t), jnp.exp2(x_s)
    et[ri, rj] = e_t
    es[ri, rj] = e_s
    diff[ri, rj] = x_t - x_s
    if i == 0:
        col[0:8, rj] = folded_sum(e_t)
        col[8:16, rj] = folded_sum(e_s)
    else:
        col[0:8, rj] += folded_sum(e_t)
        col[8:16, rj] += folded_sum(e_s)
    if j == i + 1:
        row_t[ri] = e_t[:, :128] + e_t[:, 128:]
        row_s[ri] = e_s[:, :128] + e_s[:, 128:]
    elif j > i:
        row_t[ri] += e_t[:, :128] + e_t[:, 128:]
        row_s[ri] += e_s[:, :128] + e_s[:, 128:]


def row_statistics(length, row_t, row_s, col, rvec, rb_t, rb_s, log_sum):
    valid = lax.broadcasted_iota(jnp.int32, (1, N), 1) < length
    padded = (N - length).astype(f32)

    def total(row, c):
        r = jnp.sum(row[0 : N - BL].T, axis=0, keepdims=True)
        r = jnp.concatenate([r, jnp.zeros((1, BL), f32)], axis=1)
        return jnp.where(valid, r + jnp.sum(c, axis=0, keepdims=True) - padded, 1.0)

    sum_t, sum_s = total(row_t, col[0:8]), total(row_s, col[8:16])
    r_t, r_s = jnp.where(valid, 1.0 / sum_t, 0.0), jnp.where(valid, 1.0 / sum_s, 0.0)
    rvec[0:8] = jnp.broadcast_to(r_t, (8, N))
    rvec[8:16] = jnp.broadcast_to(r_s, (8, N))
    rb_t[...] = jnp.broadcast_to(r_t, (128, N)).T
    rb_s[...] = jnp.broadcast_to(r_s, (128, N)).T
    log_sum[0:1, :] += jnp.log2(sum_s) - jnp.log2(sum_t)


def second_block(i, j, et, es, diff, rvec, rb_t, rb_s, both, kl):
    ri, rj = pl.ds(i * BL, BL), pl.ds(j * BL, BL)

    def pair(by_row, by_col):
        wide = jnp.concatenate([by_row, by_row], axis=1).reshape(BL // 8, 8, BL)
        return (wide + by_col[None]).reshape(BL, BL)

    q_t = et[ri, rj] * pair(rb_t[ri], rvec[0:8, rj])
    both[ri, rj] = (es[ri, rj] * pair(rb_s[ri], rvec[8:16, rj]) - q_t).astype(bf16)
    part = folded_sum(q_t * diff[ri, rj])
    kl[:, rj] += 0.5 * part if i == j else part


def gradient(n, weight, bt, grad, both):
    h = Head(n)
    b = head_columns(h, bt)
    scale = h.g_scale * weight
    for j in range(NB):
        lo, hi = j * BL, (j + 1) * BL
        g = dot(b[:, :hi], both[0:hi, lo:hi], NN)
        if hi < N:
            g = g + dot(b[:, hi:], both[lo:hi, hi:N], NT)
        grad[pl.ds(h.g_at, 32), lo:hi] += g * scale


def one_head(n, length, weight, ta, sb, bt, grad, lt, rt, ls, rs, et, es, diff, row_t, row_s, col, rvec, rb_t, rb_s, both, kl, log_sum):
    h = Head(n)
    right_operands(h, ta, sb, rt, rs)
    for j in range(NB):
        for i in range(j + 1):
            first_block(i, j, h, lt, rt, ls, rs, et, es, diff, row_t, row_s, col)
    row_statistics(length, row_t, row_s, col, rvec, rb_t, rb_s, log_sum)
    gradient(jnp.maximum(n - 1, 0), weight, bt, grad, both)
    for j in range(NB):
        for i in range(j + 1):
            second_block(i, j, et, es, diff, rvec, rb_t, rb_s, both, kl)


def bounded_kernel(
    lengths, weights, tq, tk, tv, sq, sk, sv, loss, top, oq, ok, ov,
    kv, rkv, rq, gq, gkv, rgkv, mine, theirs, t_sem, own_sem, send_sem, recv_sem,
    ta, sb, bt, grad, lt, rt, ls, rs, et, es, diff, row_t, row_s, col, rvec, rb_t, rb_s, both, kl, log_sum,
):
    owner, me = lax.axis_index("dp"), lax.axis_index("tensor")
    length, weight = lengths[owner], weights[owner]
    barrier = pltpu.get_barrier_semaphore()
    for s in range(1, TS):
        pl.semaphore_signal(
            barrier, inc=1, device_id={"tensor": lax.rem(me + s, TS)}, device_id_type=MESH
        )
    valid = lax.broadcasted_iota(jnp.int32, (N, 1), 0) < length
    teacher = [
        pltpu.make_async_copy(tq.at[0], ta.at[:, pl.ds(0, 1024)], t_sem.at[0]),
        pltpu.make_async_copy(tk.at[0], ta.at[:, pl.ds(1024, 128)], t_sem.at[1]),
        pltpu.make_async_copy(tv.at[0], ta.at[:, pl.ds(1152, 128)], t_sem.at[2]),
    ]
    for c in teacher:
        c.start()
    for t in range(TS):
        kv[t] = fold_kv(sk[0, :, t * 32 : t * 32 + 32], sv[0, :, t * 32 : t * 32 + 32])

    pl.semaphore_wait(barrier, TS - 1)

    def at_rows(t):
        return pl.ds(pl.multiple_of(t * ROWS, ROWS), ROWS)

    def at_lanes(t, g=0, width=256):
        return pl.ds(pl.multiple_of(t * 256 + g * 128, 128), width)

    def ends(k, t):
        return (
            lambda: (kv.at[t], rkv.at[me]),
            lambda: (sq.at[0, :, at_lanes(t)], rq.at[at_rows(me), :]),
            lambda: (gq.at[0, at_rows(t), :], oq.at[0, :, at_lanes(me, 0, 128)]),
            lambda: (gq.at[1, at_rows(t), :], oq.at[0, :, at_lanes(me, 1, 128)]),
            lambda: (gkv.at[0, t], rgkv.at[0, me]),
            lambda: (mine, theirs.at[me]),
            lambda: (gkv.at[1, t], rgkv.at[1, me]),
        )[k]()

    def remote(k, s):
        peer = lax.rem(me + s, TS)
        src, dst = ends(k, peer)
        return pltpu.make_async_remote_copy(
            src_ref=src,
            dst_ref=dst,
            send_sem=send_sem.at[k, s],
            recv_sem=recv_sem.at[k, s],
            device_id={"tensor": peer},
            device_id_type=MESH,
        )

    def own(k):
        return pltpu.make_async_copy(*ends(k, me), own_sem.at[k])

    def start(k):
        for s in range(1, TS):
            remote(k, s).start()
        own(k).start()

    def arrived(k):
        own(k).wait()
        for s in range(1, TS):
            remote(k, s).wait_recv()

    def sent(k):
        for s in range(1, TS):
            remote(k, s).wait_send()

    start(0)
    grad[...] = jnp.zeros_like(grad)
    kl[...] = jnp.zeros_like(kl)
    log_sum[...] = jnp.zeros_like(log_sum)
    both[...] = jnp.zeros_like(both)
    for c in teacher:
        c.wait()
    set_teacher(valid, ta, lt)
    arrived(0)
    start(1)
    set_student_kv(valid, rkv, sb, bt, ls)

    def leave(g):
        x = grad[128 * g : 128 * g + 128].T
        gq[g] = jnp.where(valid, x, 0.0).astype(bf16)
        start(2 + g)

    quarter = ROWS // 4

    def leave_kv(i):
        x = jnp.concatenate([grad[256 + 32 * i : 288 + 32 * i], jnp.zeros((96, N), f32)], axis=0).T
        x = jnp.where(valid, x, 0.0).astype(bf16).reshape(TS, 4, quarter, 128)
        gkv[i] = jnp.concatenate([x[:, r, :, 0:32] for r in range(4)], axis=2)
        start(4 + 2 * i)

    def take_kv(i, out):
        arrived(4 + 2 * i)
        for r in range(4):
            out[0, r * quarter : (r + 1) * quarter, :] = jnp.concatenate(
                [rgkv[i, t][:, 32 * r : 32 * r + 32] for t in range(TS)], axis=1
            )

    def step(n, carry):
        @pl.when(n == HEADS)
        def _():
            arrived(1)
            set_student_q(valid, rq, sb, bt, ls)
            mine[...] = jnp.maximum(
                jnp.maximum(bound_lanes(ta[:, 0:1024], 128), bound_lanes(ta[:, 1024:1280], 16)),
                jnp.maximum(bound_lanes(sb[:, 0:256], 32), bound_lanes(sb[:, 256:512], 4)),
            )
            start(5)

        @pl.when(n == HEADS + 1)
        def _():
            leave_kv(0)

        @pl.when(n == 2 * HEADS)
        def _():
            take_kv(0, ok)

        @pl.when(n == HEADS + 5)
        def _():
            leave(0)

        @pl.when(n == HEADS + 9)
        def _():
            leave(1)

        one_head(n, length, weight, ta, sb, bt, grad, lt, rt, ls, rs, et, es, diff, row_t, row_s, col, rvec, rb_t, rb_s, both, kl, log_sum)
        return carry

    lax.fori_loop(0, 3 * HEADS, step, 0)
    gradient(3 * HEADS - 1, weight, bt, grad, both)
    leave_kv(1)
    total = (jnp.sum(kl[...]) + jnp.sum(log_sum[...])) * math.log(2.0)
    loss[0, 0] = total / length.astype(f32)
    arrived(5)
    top[0, 0] = jnp.max(theirs[...])
    arrived(2)
    arrived(3)
    take_kv(1, ov)
    for k in range(7):
        sent(k)


def bounded_program(tq, tk, tv, sq, sk, sv, lengths, weights):
    smem = pl.BlockSpec(memory_space=pltpu.SMEM)
    vmem = pl.BlockSpec(memory_space=pltpu.VMEM)
    hbm = pl.BlockSpec(memory_space=pl.ANY)
    square = (N, N)
    message = (TS, HALF, 128)
    return pl.pallas_call(
        bounded_kernel,
        out_shape=(
            jax.ShapeDtypeStruct((1, 1), f32),
            jax.ShapeDtypeStruct((1, 1), f32),
            jax.ShapeDtypeStruct((1, ROWS, 2048), bf16),
            jax.ShapeDtypeStruct((1, ROWS, 256), bf16),
            jax.ShapeDtypeStruct((1, ROWS, 256), bf16),
        ),
        in_specs=[smem, smem, hbm, hbm, hbm, hbm, vmem, vmem],
        out_specs=[smem, smem, hbm, vmem, vmem],
        scratch_shapes=[
            pltpu.VMEM(message, bf16),
            pltpu.VMEM(message, bf16),
            pltpu.VMEM((N, 256), bf16),
            pltpu.VMEM((2, N, 128), bf16),
            pltpu.VMEM((2, TS, ROWS // 4, 128), bf16),
            pltpu.VMEM((2, TS, ROWS // 4, 128), bf16),
            pltpu.VMEM((8, 128), f32),
            pltpu.VMEM((TS, 8, 128), f32),
            pltpu.SemaphoreType.DMA((3,)),
            pltpu.SemaphoreType.DMA((7,)),
            pltpu.SemaphoreType.DMA((7, TS)),
            pltpu.SemaphoreType.DMA((7, TS)),
            pltpu.VMEM((N, 1280), bf16),
            pltpu.VMEM((N, 512), bf16),
            pltpu.VMEM((320, N), bf16),
            pltpu.VMEM((320, N), f32),
            pltpu.VMEM((HEADS + 2, N, 256), bf16),
            pltpu.VMEM((N, 128), bf16),
            pltpu.VMEM((4, N, 256), bf16),
            pltpu.VMEM((N, 128), bf16),
            pltpu.VMEM(square, f32),
            pltpu.VMEM(square, f32),
            pltpu.VMEM(square, f32),
            pltpu.VMEM((N, 128), f32),
            pltpu.VMEM((N, 128), f32),
            pltpu.VMEM((16, N), f32),
            pltpu.VMEM((16, N), f32),
            pltpu.VMEM((N, 128), f32),
            pltpu.VMEM((N, 128), f32),
            pltpu.VMEM(square, bf16),
            pltpu.VMEM((8, N), f32),
            pltpu.VMEM((8, N), f32),
        ],
        compiler_params=pltpu.CompilerParams(
            collective_id=0, has_side_effects=True, vmem_limit_bytes=VMEM_LIMIT
        ),
        cost_estimate=pl.CostEstimate(
            flops=40 * 10**9, bytes_accessed=4 * 10**6, transcendentals=32 * 10**6
        ),
    )(lengths, weights, tq, tk, tv, sq, sk, sv)


def keep_kernel(loss, q, k, v, loss_out, q_out, k_out, v_out, sem):
    pairs = ((q, q_out), (k, k_out), (v, v_out))
    copies = [pltpu.make_async_copy(a, b, sem.at[i]) for i, (a, b) in enumerate(pairs)]
    for c in copies:
        c.start()
    loss_out[0, 0] = loss[0, 0]
    for c in copies:
        c.wait()


def keep(*results):
    specs = [pl.BlockSpec(memory_space=pltpu.SMEM)] + [pl.BlockSpec(memory_space=pl.ANY)] * 3
    return pl.pallas_call(
        keep_kernel,
        out_shape=[jax.ShapeDtypeStruct(r.shape, r.dtype) for r in results],
        in_specs=specs,
        out_specs=specs,
        scratch_shapes=[pltpu.SemaphoreType.DMA((3,))],
    )(*results)


def on_device(*arrays):
    loss, bound, *gradients = bounded_program(*arrays)
    return lax.cond(
        bound[0, 0] <= SAFE_LOG2,
        lambda: tuple(keep(loss, *gradients)),
        lambda: general_program(*arrays),
    )


def solution(mesh):
    in_specs = (
        P("dp", None, "tensor"),
        P("dp", None, "tensor"),
        P("dp", None, "tensor"),
        P("dp", "tensor", None),
        P("dp", "tensor", None),
        P("dp", "tensor", None),
        P(),
        P(),
    )
    out_specs = (
        P("dp", "tensor"),
        P("dp", "tensor", None),
        P("dp", "tensor", None),
        P("dp", "tensor", None),
    )
    return jax.shard_map(
        on_device, mesh=mesh, in_specs=in_specs, out_specs=out_specs, check_vma=False
    )
```
